128 devices in a mesh: face: 4 (over y), patch: 32 (over x, z, core).
Axes of the slice: x: 4, y: 4, z: 4, core: 2. Of those that a mesh axis runs over, the one named last changes fastest.
Arguments:
- coarse: bfloat16 [128, 512, 512], P(None, 'patch', 'face'), may hold values from -6 to 6
- w_up: bfloat16 [3, 3, 64, 128], replicated, may hold values from -0.375 to 0.375
- w_mix: bfloat16 [3, 3, 64, 64], replicated, may hold values from -0.25 to 0.25
- w_head: float32 [8, 64], replicated, may hold values from -0.75 to 0.75
- send_index: int32 [4, 128, 4096], P('face', 'patch'), may hold values from 0 to 8191, as said below
- slot_ids: int32 [4, 2097152], P(None, ('face', 'patch')), may hold values from 0 to 16383, as said below
- fractions: float32 [2, 2097152], P(None, ('face', 'patch')), may hold values from 0 to 1
- head_cot: float32 [8, 2097152], P(None, ('face', 'patch')), may hold values from -0.01171875 to 0.01171875
Outputs:
- head: float32 [8, 2097152], P(None, ('face', 'patch'))
- up_grad: float32 [3, 3, 64, 128], replicated
- mix_grad: float32 [3, 3, 64, 64], replicated
- head_grad: float32 [8, 64], replicated
The draws below stay inside these ranges and needn't reach their ends.
Inputs may be any that keep to these rules, and one draw needn't show every extreme that they name: `send_index`: each row s * 4 + r lists a run of whole consecutive pixel columns of the source, starting at a column boundary, of 2 to 16 columns, its last entry repeated in the slots after the run; for r = 3 the run fills 4096 slots and ends at the block's last pixel, for r = 2 it fills 4096 slots, for smaller r it starts at pixel 0. `slot_ids`: A point's four slots are t, t + 1, t + 256, t + 257 for corners 0..3, all within one run of live slots of one r, and t not in a run's last row.
All inputs are finite; a program needn't handle non-finite values.
Results may differ from the reference program's by a relative error of at most 0.0047.
Values may be sent and summed in bfloat16 or wider, within the bound.
A program may use at most 128 MiB of HBM per device.

```python
import jax
import jax.numpy as jnp
from jax import lax

CIN = 128
CF = 64
COUT = 8
REACH = 4
HF_DEV = 256
WF_DEV = 32
LL_DEV = 16384
CAP = 4096
FINE_ROWS = 1024
FINE_COLS = 1024
POINTS = 2097152
N_FACE = 4
N_PATCH = 32


def route_plan(key):
    base = jax.random.fold_in(key, 7)
    first_key, second_key = jax.random.split(base)
    col_cap = CAP // HF_DEV
    lowest = max(2, col_cap // 4)
    shape = (N_FACE, N_PATCH, REACH)
    columns = jax.random.randint(first_key, shape, lowest, col_cap + 1)
    which = lax.broadcasted_iota(jnp.int32, shape, 2)
    columns = jnp.where(which >= REACH - 2, col_cap, columns)
    counts = columns * HF_DEV
    own_start = jax.random.randint(second_key, shape, 0, WF_DEV - col_cap + 1) * HF_DEV
    pixels = HF_DEV * WF_DEV
    starts = jnp.where(which == REACH - 1, pixels - counts, jnp.where(which == REACH - 2, own_start, 0))
    return (counts.astype(jnp.int32), starts.astype(jnp.int32))


def draw_send_index(key, part):
    counts, starts = route_plan(key)
    position = jnp.arange(CAP, dtype=jnp.int32)
    index = starts[..., None] + jnp.minimum(position, counts[..., None] - 1)
    return index.reshape(N_FACE, N_PATCH * REACH, CAP).astype(jnp.int32)


def draw_slot_ids(key, part):
    counts, starts = route_plan(key)
    pick_key = jax.random.fold_in(key, 11)
    which_key, column_key, row_key = jax.random.split(pick_key, 3)
    point = jnp.arange(POINTS, dtype=jnp.int32)
    device = point // LL_DEV
    face_of = device // N_PATCH
    patch_of = device % N_PATCH
    leading = point % LL_DEV == 0
    which = jnp.where(leading, REACH - 1, jax.random.randint(which_key, (POINTS,), 0, REACH))
    source = (patch_of + N_PATCH + REACH - 2 - which) % N_PATCH
    columns = counts[face_of, source, which] // HF_DEV
    column = jax.random.randint(column_key, (POINTS,), 0, 1048576) % (columns - 1)
    row = jax.random.randint(row_key, (POINTS,), 0, HF_DEV - 1)
    column = jnp.where(leading, columns - 2, column)
    row = jnp.where(leading, HF_DEV - 2, row)
    corner = which * CAP + column * HF_DEV + row
    return jnp.stack([corner, corner + 1, corner + HF_DEV, corner + HF_DEV + 1], axis=0).astype(jnp.int32)


def block_levels(own_key, shape, cuts, smallest, largest):
    gain, own = 1.0, jax.random.fold_in(own_key, 6)
    for dim, blocks in cuts:
        draws = jnp.exp(jax.random.uniform(jax.random.fold_in(own, dim), (blocks,), jnp.float32, smallest / len(cuts), largest / len(cuts)))
        gain = gain * jnp.repeat(draws, shape[dim] // blocks).reshape([-1 if axis == dim else 1 for axis in range(len(shape))])
    return gain


def centred(rng, dims, scale, most, cuts=(), kind=jnp.bfloat16):
    array = jax.random.normal(rng, dims, jnp.float32) * scale
    if len(cuts) > 0:
        array = block_levels(rng, dims, cuts, -0.22, 0.18) * array
    return jnp.clip(array, min=-most, max=most).astype(kind)


def setup_inputs(seed: int = 0) -> dict:
    key_list = jax.random.split(jax.random.key(seed), 9)
    coarse = centred(key_list[0], (CIN, FINE_COLS // 2, FINE_ROWS // 2), 1.0, 6.0, ((1, 32), (2, 4)))
    w_up = centred(key_list[1], (3, 3, CF, CIN), (2 * CIN) ** -0.5, 0.375)
    w_mix = centred(key_list[2], (3, 3, CF, CF), (9 * CF) ** -0.5, 0.25)
    w_head = centred(key_list[3], (COUT, CF), CF ** -0.5, 0.75, (), jnp.float32)
    send_index = draw_send_index(jax.random.fold_in(key_list[8], 71), 0)
    slot_ids = draw_slot_ids(jax.random.fold_in(key_list[8], 71), 0)
    fractions = jnp.clip(1.0 * jax.random.uniform(key_list[6], (2, POINTS), jnp.float32) ** block_levels(key_list[6], (2, POINTS), ((1, 128),), -0.2, 0.2), 0.0, 1.0)
    head_cot = centred(key_list[7], (COUT, POINTS), 0.002, 0.01171875, ((1, 128),), jnp.float32)
    return {"coarse": coarse, "w_up": w_up, "w_mix": w_mix, "w_head": w_head, "send_index": send_index, "slot_ids": slot_ids, "fractions": fractions, "head_cot": head_cot}


PAIRS = (((1, 0),), ((2, 0), (0, 1)))

def matmul_taps(weight, window):
    channels = window.shape[0]
    flat = window.reshape(channels, -1)
    result = jnp.dot(weight, flat, preferred_element_type=jnp.float32)
    return result.reshape((weight.shape[0],) + window.shape[1:])

def tap_grad(grad_window, window):
    left = grad_window.reshape(grad_window.shape[0], -1)
    right = window.reshape(window.shape[0], -1)
    return lax.dot_general(left, right, (((1,), (1,)), ((), ())), preferred_element_type=jnp.float32)

def up_convolve(extended, w_up):
    narrow = extended.shape[1] - 1
    short = extended.shape[2] - 1
    outer = w_up.shape[2]
    columns = []
    for col_parity in range(2):
        row_parts = []
        for row_parity in range(2):
            summed = jnp.zeros((outer, narrow, short), jnp.float32)
            for col_tap, col_shift in PAIRS[col_parity]:
                for row_tap, row_shift in PAIRS[row_parity]:
                    window = extended[:, col_shift:col_shift + narrow, row_shift:row_shift + short]
                    summed = summed + matmul_taps(w_up[col_tap, row_tap], window)
            row_parts.append(summed)
        columns.append(jnp.stack(row_parts, axis=3).reshape(outer, narrow, 2 * short))
    return jnp.stack(columns, axis=2).reshape(outer, 2 * narrow, 2 * short)

def up_weight_grad(grad_fine, extended):
    outer = grad_fine.shape[0]
    narrow = extended.shape[1] - 1
    short = extended.shape[2] - 1
    split = grad_fine.reshape(outer, narrow, 2, short, 2)
    table = [[None, None, None] for number in range(3)]
    for col_parity in range(2):
        for row_parity in range(2):
            parity_part = split[:, :, col_parity, :, row_parity]
            for col_tap, col_shift in PAIRS[col_parity]:
                for row_tap, row_shift in PAIRS[row_parity]:
                    window = extended[:, col_shift:col_shift + narrow, row_shift:row_shift + short]
                    table[col_tap][row_tap] = tap_grad(parity_part, window)
    return jnp.stack([jnp.stack(table[number], axis=0) for number in range(3)], axis=0)

def convolve(padded, weight):
    wide = padded.shape[1] - 2
    tall = padded.shape[2] - 2
    summed = jnp.zeros((weight.shape[2], wide, tall), jnp.float32)
    for col_tap in range(3):
        for row_tap in range(3):
            window = padded[:, col_tap:col_tap + wide, row_tap:row_tap + tall]
            summed = summed + matmul_taps(weight[col_tap, row_tap], window)
    return summed

def convolve_back(padded, weight):
    wide = padded.shape[1] - 2
    tall = padded.shape[2] - 2
    summed = jnp.zeros((weight.shape[3], wide, tall), jnp.float32)
    for col_tap in range(3):
        for row_tap in range(3):
            window = padded[:, 2 - col_tap:2 - col_tap + wide, 2 - row_tap:2 - row_tap + tall]
            summed = summed + matmul_taps(weight[col_tap, row_tap].T, window)
    return summed

def conv_weight_grad(grad_out, padded):
    wide = padded.shape[1] - 2
    tall = padded.shape[2] - 2
    table = []
    for col_tap in range(3):
        line = []
        for row_tap in range(3):
            line.append(tap_grad(grad_out, padded[:, col_tap:col_tap + wide, row_tap:row_tap + tall]))
        table.append(jnp.stack(line, axis=0))
    return jnp.stack(table, axis=0)

def swish(value):
    return value * jax.nn.sigmoid(value)

def swish_slope(value):
    sigma = jax.nn.sigmoid(value)
    return sigma * (1.0 + value * (1.0 - sigma))

def bilinear(fractions):
    along = fractions[0]
    across = fractions[1]
    return jnp.stack([(1.0 - along) * (1.0 - across), along * (1.0 - across), (1.0 - along) * across, along * across], axis=0)

def interpolate(values, slot_ids, weights):
    summed = weights[0] * jnp.take(values, slot_ids[0], axis=1).astype(jnp.float32)
    for corner in range(1, 4):
        summed = summed + weights[corner] * jnp.take(values, slot_ids[corner], axis=1).astype(jnp.float32)
    return summed

def spread(values, slot_ids, weights, count):
    summed = jnp.zeros((values.shape[0], count), jnp.float32)
    for corner in range(4):
        summed = summed.at[:, slot_ids[corner]].add(weights[corner] * values)
    return summed

def pad_fine(value):
    value = jnp.pad(value, ((0, 0), (0, 0), (1, 1)))
    return jnp.concatenate([value[:, -1:, :], value, value[:, :1, :]], axis=1)

def inner_rows(left, right):
    return lax.dot_general(left, right, (((1,), (1,)), ((), ())), precision=lax.Precision.HIGHEST, preferred_element_type=jnp.float32)

def reference(coarse, w_up, w_mix, w_head, send_index, slot_ids, fractions, head_cot):
    taller = jnp.concatenate([coarse, jnp.zeros_like(coarse[:, :, :1])], axis=2)
    extended = jnp.concatenate([taller, taller[:, :1, :]], axis=1)
    first = up_convolve(extended, w_up)
    hidden = swish(first).astype(jnp.bfloat16)
    hidden_pad = pad_fine(hidden)
    second = convolve(hidden_pad, w_mix)
    features = swish(second).astype(jnp.bfloat16)
    devices = N_FACE * N_PATCH
    pixels = HF_DEV * WF_DEV
    blocks = features.reshape(CF, N_PATCH, WF_DEV, N_FACE, HF_DEV).transpose(3, 1, 0, 2, 4).reshape(N_FACE, N_PATCH, CF, pixels)
    plan = send_index.reshape(N_FACE, N_PATCH, REACH * CAP)
    picker = jax.vmap(jax.vmap(lambda block, where: jnp.take(block, where, axis=1)))
    sent = picker(blocks, plan).reshape(N_FACE, N_PATCH, CF, REACH, CAP)
    pieces = [jnp.roll(sent[:, :, :, number], -(REACH - 2 - number), axis=1) for number in range(REACH)]
    arrived = jnp.stack(pieces, axis=3).reshape(devices, CF, REACH * CAP)
    slots = slot_ids.reshape(4, devices, LL_DEV).transpose(1, 0, 2)
    shares = fractions.reshape(2, devices, LL_DEV).transpose(1, 0, 2)
    cotans = head_cot.reshape(COUT, devices, LL_DEV).transpose(1, 0, 2)

    def per_device(items):
        values, slot, share, cotan = items
        weights = bilinear(share)
        sampled = interpolate(values, slot, weights)
        result = jnp.dot(w_head, sampled, precision=lax.Precision.HIGHEST)
        feat_cot = jnp.dot(w_head.T, cotan, precision=lax.Precision.HIGHEST)
        slot_cot = spread(feat_cot, slot, weights, REACH * CAP)
        return (result, slot_cot, inner_rows(cotan, sampled))
    heads, slot_cots, partials = lax.map(per_device, (arrived, slots, shares, cotans))
    head = heads.transpose(1, 0, 2).reshape(COUT, POINTS)
    head_grad = lax.optimization_barrier(jnp.sum(partials, axis=0))
    slot_blocks = slot_cots.reshape(N_FACE, N_PATCH, CF, REACH, CAP)
    backs = [jnp.roll(slot_blocks[:, :, :, number], REACH - 2 - number, axis=1) for number in range(REACH)]
    returned = jnp.stack(backs, axis=3).reshape(N_FACE, N_PATCH, CF, REACH * CAP)

    def scatter_back(values, where):
        return jnp.zeros((CF, pixels), jnp.float32).at[:, where].add(values)
    pixel_cot = jax.vmap(jax.vmap(scatter_back))(returned, plan)
    fine_cot = pixel_cot.reshape(N_FACE, N_PATCH, CF, WF_DEV, HF_DEV).transpose(2, 1, 3, 0, 4).reshape(CF, FINE_COLS, FINE_ROWS)
    second_cot = (fine_cot * swish_slope(second)).astype(jnp.bfloat16)
    mix_grad = conv_weight_grad(second_cot, hidden_pad)
    hidden_cot = convolve_back(pad_fine(second_cot), w_mix)
    first_cot = (hidden_cot * swish_slope(first)).astype(jnp.bfloat16)
    up_grad = up_weight_grad(first_cot, extended)
    return (head, up_grad, mix_grad, head_grad)
```

```python
import functools

import jax
import jax.numpy as jnp
from jax import lax
from jax.experimental import pallas as pl
from jax.experimental.pallas import tpu as pltpu
from jax.sharding import PartitionSpec as P

MESH = pl.DeviceIdType.MESH
F32 = jnp.float32
BF16 = jnp.bfloat16

LANES = 128
CIN = 128
CF = 64
COUT = 8
COLS = 16
POINT_TILE = 512
GRAD_ROWS = 1024
MIX_ROW = 9 * CF
HEAD_ROW = MIX_ROW + 6 * CF
NEIGHBOURS = tuple((df, dp) for df in (-1, 0, 1) for dp in (-1, 0, 1) if (df, dp) != (0, 0))
ROW_NEIGHBOURS = tuple(pair for pair in NEIGHBOURS if pair[0] != 0)


def dot(left, right):
    return lax.dot_general(left, right, (((1,), (0,)), ((), ())), preferred_element_type=F32)


def dot_nt(left, right):
    return lax.dot_general(left, right, (((1,), (1,)), ((), ())), preferred_element_type=F32)


def turn(value, steps):
    if isinstance(steps, int):
        steps = steps % LANES
        if steps == 0:
            return value
    return pltpu.roll(value, steps, axis=1)


def sigmoid(value):
    return 0.5 * jnp.tanh(0.5 * value) + 0.5


def row_weights(slot, along):
    width = slot.shape[1]
    place = lax.broadcasted_iota(jnp.int32, (256, width), 0)
    natural = 2 * (place & 127) + (place >> 7)
    away = natural - (slot & 255)
    weight = jnp.where(away == 0, 1.0 - along, jnp.where(away == 1, along, 0.0))
    return weight.astype(BF16)


def local_kernel(
    nf, npat,
    start_ref, coarse_ref, edge_ref, wup_ref, wmix_ref, wback_ref, whead_ref, wheadt_ref,
    slot_ref, frac_ref, cot_ref,
    head_ref, grad_ref,
    ext, exts, edges, upw, hid, slope1, slope2, feat, gown, gsend, table,
    sacc, srecv, pad, sc, strip, strips, zbuf, fc, mixacc, upacc,
    send_sem, recv_sem,
):
    me_f, me_p = lax.axis_index("face"), lax.axis_index("patch")

    def device(df, dp):
        return (lax.rem(me_f + df + nf, nf), lax.rem(me_p + dp + npat, npat))

    barrier = pltpu.get_barrier_semaphore()
    partners = NEIGHBOURS + ((0, 2), (0, -2))
    for df, dp in partners:
        pl.semaphore_signal(barrier, inc=1, device_id=device(df, dp), device_id_type=MESH)
    pl.semaphore_wait(barrier, len(partners))

    copies = []

    def send(source, target, offset):
        number = len(copies)
        copy = pltpu.make_async_remote_copy(
            src_ref=source, dst_ref=target,
            send_sem=send_sem.at[number], recv_sem=recv_sem.at[number],
            device_id=device(*offset), device_id_type=MESH,
        )
        copy.start()
        copies.append(copy)
        return copy

    coarse_copies = [
        send(coarse_ref.at[0], ext.at[COLS + 1], (0, -1)),
        send(coarse_ref.at[COLS - 1], ext.at[0], (0, 1)),
    ]
    for number, offset in enumerate(NEIGHBOURS):
        coarse_copies.append(send(edge_ref, edges.at[number], offset))

    ext[1 : COLS + 1] = coarse_ref[...]
    ext[COLS + 2] = jnp.zeros((CIN, LANES), BF16)
    for row_tap in range(3):
        low = slice(row_tap * CF, (row_tap + 1) * CF)
        high = slice((3 + row_tap) * CF, (4 + row_tap) * CF)
        upw[low, :CIN] = wup_ref[1, row_tap]
        upw[low, CIN:] = jnp.zeros((CF, CIN), BF16)
        upw[high, :CIN] = wup_ref[2, row_tap]
        upw[high, CIN:] = wup_ref[0, row_tap]

    sacc[...] = jnp.zeros_like(sacc)

    @pl.loop(0, slot_ref.shape[1] // POINT_TILE)
    def _(step):
        here = pl.ds(pl.multiple_of(step * POINT_TILE, POINT_TILE), POINT_TILE)
        slot = slot_ref[0:1, here]
        along, across = frac_ref[0:1, here], frac_ref[1:2, here]
        rows = row_weights(slot, along)
        cot = cot_ref[:, here]
        near, far = cot * (1.0 - across), cot * across
        column = jnp.broadcast_to(slot >> 8, near.shape)[None]
        number = lax.broadcasted_iota(jnp.int32, (64,) + near.shape, 0)
        away = number - column
        terms = jnp.where(away == 0, near[None], jnp.where(away == 1, far[None], 0.0))
        sacc[...] += dot_nt(terms.reshape(64 * COUT, POINT_TILE).astype(BF16), rows)

    run = COLS * COUT
    pad[0:16] = jnp.zeros((16, COUT, 256), F32)
    pad[16:32] = sacc[2 * run : 3 * run].reshape(16, COUT, 256)
    pad[32:48] = jnp.zeros((16, COUT, 256), F32)
    back_copies = [
        send(sacc.at[0:run], srecv.at[0], (0, 2)),
        send(sacc.at[run : 2 * run], srecv.at[1], (0, 1)),
        send(sacc.at[3 * run : 4 * run], srecv.at[2], (0, -1)),
    ]

    for copy in coarse_copies:
        copy.wait_recv()
    lane = lax.broadcasted_iota(jnp.int32, (CIN, LANES), 1)
    lane64 = lane[:CF]
    above = jnp.where(me_f > 0, 1.0, 0.0).astype(F32)
    below = jnp.where(me_f < nf - 1, 1.0, 0.0).astype(F32)

    def arrived(buffer, df, dp):
        pairs = NEIGHBOURS if buffer is edges else ROW_NEIGHBOURS
        return buffer[pairs.index((-df, -dp))].astype(F32)

    def between(low, high, index):
        return jnp.logical_and(index >= low, index < high)

    top = jnp.where(between(1, 17, lane), turn(arrived(edges, -1, 0), -15), 0.0)
    top = jnp.where(lane == 0, turn(arrived(edges, -1, -1), -31), top)
    top = jnp.where(lane == 17, turn(arrived(edges, -1, 1), 1), top) * above
    first_row = jnp.where(between(33, 49, lane), turn(edge_ref[...].astype(F32), 33), 0.0)
    first_row = jnp.where(lane == 32, turn(arrived(edges, 0, -1), 17), first_row)
    first_row = jnp.where(lane == 49, turn(arrived(edges, 0, 1), 49), first_row)
    bottom = jnp.where(between(65, 81, lane), turn(arrived(edges, 1, 0), 65), 0.0)
    bottom = jnp.where(lane == 64, turn(arrived(edges, 1, -1), 49), bottom)
    bottom = jnp.where(lane == 81, turn(arrived(edges, 1, 1), 81), bottom) * below
    rim = top + first_row + bottom
    rim_pair = jnp.concatenate([rim, turn(rim, -1)], axis=0).astype(BF16)
    rim_out = dot(upw[...], rim_pair)
    rim_hidden = []
    for parity in range(2):
        part = rim_out[parity * 192 : (parity + 1) * 192]
        upper = part[128:192] + turn(part[0:64], -32)
        value = jnp.where(lane64 < 32, upper * above, jnp.where(between(64, 96, lane64), part[64:128], 0.0))
        rim_hidden.append(value * sigmoid(value))
    even_rim, odd_rim = rim_hidden
    mix_rim = [
        dot(wmix_ref[...], jnp.concatenate([turn(odd_rim, 1), even_rim, odd_rim], axis=0).astype(BF16)),
        dot(wmix_ref[...], jnp.concatenate([even_rim, odd_rim, turn(even_rim, -1)], axis=0).astype(BF16)),
    ]

    @pl.loop(0, 9)
    def _(step):
        t = 2 * step
        pair = [ext[pl.ds(t + k, 2)].reshape(2 * CIN, LANES) for k in range(2)]
        out = dot(upw[...], jnp.concatenate(pair, axis=1))
        for k in range(2):
            here = t + k
            for parity in range(2):
                part = out[parity * 192 : (parity + 1) * 192, k * LANES : (k + 1) * LANES]
                entering = turn(rim_out[parity * 192 : parity * 192 + 64], 63 - here)
                odd = part[128:192] + jnp.where(lane64 == 127, entering, turn(part[0:64], -1))
                value = jnp.concatenate([part[64:128], odd], axis=1)
                sigma = sigmoid(value)
                hid[2 * here + parity] = (value * sigma).astype(BF16)
                slope1[2 * here + parity] = sigma * (1.0 + value * (1.0 - sigma))
            shifted = turn(ext[here].astype(F32), -1)
            exts[here] = jnp.where(lane == 127, turn(rim, 63 - here), shifted).astype(BF16)

    weight = whead_ref[...]
    weight_high = weight.astype(BF16).astype(F32)
    head_pair = jnp.concatenate([weight_high, weight - weight_high], axis=0).astype(BF16)

    def mix_step(j):
        values = []
        for parity in range(2):
            q = 2 * j + parity
            out = dot(wmix_ref[...], hid[pl.ds(q + 1, 3)].reshape(192, 256))
            low, mid, high = out[0:64], out[64:128], out[128:192]
            first = turn(mix_rim[parity][0:64], 127 - j)
            last = turn(mix_rim[parity][128:192], 62 - j)
            even = jnp.where(lane64 == 0, first, turn(low[:, LANES:], 1)) + mid[:, :LANES] + high[:, LANES:]
            odd = low[:, :LANES] + mid[:, LANES:] + jnp.where(lane64 == 127, last, turn(high[:, :LANES], -1))
            value = jnp.concatenate([even, odd], axis=1)
            sigma = sigmoid(value)
            feature = (value * sigma).astype(BF16)
            feat[q] = feature
            slope2[q] = sigma * (1.0 + value * (1.0 - sigma))
            both = dot(head_pair, feature)
            point_value = both[0:8] + both[8:16]
            gown[q] = point_value
            values.append(point_value)
        gsend[j] = jnp.concatenate(values, axis=0).astype(BF16)

    pl.loop(0, 8)(mix_step)
    value_copies = [
        send(gsend.at[0:8], table.at[0:8], (0, -2)),
        send(gsend.at[0:8], table.at[8:16], (0, -1)),
    ]
    pl.loop(8, 16)(mix_step)
    value_copies.append(send(gsend.at[8:16], table.at[24:32], (0, 1)))

    start = start_ref[0]
    for k in range(8):
        pair = [gown[start + 2 * k], gown[start + 2 * k + 1]]
        table[16 + k] = jnp.concatenate(pair, axis=0).astype(BF16)

    for copy in back_copies:
        copy.wait_recv()
    weight_t = wheadt_ref[...]
    high_t = weight_t.astype(BF16).astype(F32)
    weight_three = jnp.concatenate([high_t, weight_t - high_t, high_t], axis=1).astype(BF16)
    strip[...] = jnp.zeros_like(strip)

    def cot_step(q, total, head_sum):
        high = total.astype(BF16).astype(F32)
        low = total - high
        fine = dot(weight_three, jnp.concatenate([high, high, low], axis=0).astype(BF16))
        value = fine * slope2[q]
        sc[q + 1] = value.astype(BF16)
        kept = jnp.where(lane64 == q, turn(value[:, :LANES], q), strip[...])
        strip[...] = jnp.where(lane64 == q + 32, turn(value[:, LANES:], q + 33), kept)
        both = dot_nt(jnp.concatenate([high, low], axis=0).astype(BF16), feat[q])
        return head_sum + both[0:8] + both[8:16]

    def row_of(number, q):
        return srecv[number, pl.ds(pl.multiple_of(q * COUT, COUT), COUT), :]

    def cot_low(q, head_sum):
        total = row_of(0, q) + row_of(1, q) + pad[16 + q - start]
        return cot_step(q, total, head_sum)

    def cot_high(q, head_sum):
        total = row_of(2, q - 16) + pad[16 + q - start]
        return cot_step(q, total, head_sum)

    head_sum = lax.fori_loop(0, 16, cot_low, jnp.zeros((COUT, CF), F32))
    head_sum = lax.fori_loop(16, 32, cot_high, head_sum)
    strips_own = strips.at[len(ROW_NEIGHBOURS)]
    strips_own[...] = strip[...].astype(BF16)
    cot_copies = [
        send(sc.at[1], sc.at[33], (0, -1)),
        send(sc.at[32], sc.at[0], (0, 1)),
    ]
    for number, offset in enumerate(ROW_NEIGHBOURS):
        cot_copies.append(send(strips_own, strips.at[number], offset))

    for copy in value_copies:
        copy.wait_recv()

    @pl.loop(0, slot_ref.shape[1] // POINT_TILE)
    def _(step):
        here = pl.ds(pl.multiple_of(step * POINT_TILE, POINT_TILE), POINT_TILE)
        slot = slot_ref[0:1, here]
        along, across = frac_ref[0:1, here], frac_ref[1:2, here]
        rows = row_weights(slot, along)
        columns = dot(table[...].reshape(64 * COUT, 256), rows).reshape(64, COUT, POINT_TILE)
        column = jnp.broadcast_to(slot >> 8, (COUT, POINT_TILE))[None]
        number = lax.broadcasted_iota(jnp.int32, (64, COUT, POINT_TILE), 0)
        away = number - column
        near = jnp.broadcast_to(1.0 - across, (COUT, POINT_TILE))[None]
        far = jnp.broadcast_to(across, (COUT, POINT_TILE))[None]
        weights = jnp.where(away == 0, near, jnp.where(away == 1, far, 0.0))
        head_ref[:, here] = jnp.sum(weights * columns, axis=0)

    for copy in cot_copies:
        copy.wait_recv()
    upper = jnp.where(between(1, 33, lane64), turn(arrived(strips, -1, 0), -31), 0.0)
    upper = jnp.where(lane64 == 0, turn(arrived(strips, -1, -1), -63), upper)
    upper = jnp.where(lane64 == 33, turn(arrived(strips, -1, 1), 1), upper) * above
    lower = jnp.where(between(65, 97, lane64), turn(arrived(strips, 1, 0), 65), 0.0)
    lower = jnp.where(lane64 == 64, turn(arrived(strips, 1, -1), 33), lower)
    lower = jnp.where(lane64 == 97, turn(arrived(strips, 1, 1), 97), lower) * below
    cot_rim = upper + lower

    def back_step(w):
        value = sc[w].astype(F32)
        even, odd = value[:, :LANES], value[:, LANES:]
        last = jnp.where(lane64 == 127, turn(cot_rim, 63 - w), turn(even, -1))
        first = jnp.where(lane64 == 0, turn(cot_rim, LANES - w), turn(odd, 1))
        taps = jnp.concatenate(
            [jnp.concatenate([odd, last], axis=1), value, jnp.concatenate([first, even], axis=1)],
            axis=0,
        ).astype(BF16)
        zbuf[w] = dot(wback_ref[...], taps)
        return taps

    mixacc[...] = jnp.zeros_like(mixacc)
    back_step(0)

    @pl.loop(1, 33)
    def _(w):
        taps = back_step(w)
        mixacc[...] += dot_nt(taps, hid[pl.ds(w, 3)].reshape(192, 256))

    back_step(33)

    upacc[...] = jnp.zeros_like(upacc)

    @pl.loop(0, 8)
    def _(step):
        evens, odds = [], []
        for k in range(2):
            even_parts, odd_parts = [], []
            for parity in range(2):
                q = 4 * step + 2 * k + parity
                total = zbuf[q + 2, 0:64] + zbuf[q + 1, 64:128] + zbuf[q, 128:192]
                value = (total * slope1[q + 2]).astype(BF16)
                even_parts.append(value[:, :LANES])
                odd_parts.append(value[:, LANES:])
            evens.append(jnp.concatenate(even_parts, axis=0))
            odds.append(jnp.concatenate(odd_parts, axis=0))
        even = jnp.concatenate(evens, axis=1)
        odd = jnp.concatenate(odds, axis=1)

        def window(buffer):
            pair = [buffer[pl.ds(2 * step + 1 + k, 2)].reshape(2 * CIN, LANES) for k in range(2)]
            return jnp.concatenate(pair, axis=1)

        plain, moved = window(ext), window(exts)
        upacc[0] += dot_nt(odd, moved)
        upacc[1] += dot_nt(even, plain)
        upacc[2] += dot_nt(odd, plain)

    for row_tap in range(3):
        for col_tap, rows, lanes in ((0, 64, 128), (1, 0, 0), (2, 64, 0)):
            at = (col_tap * 3 + row_tap) * CF
            grad_ref[at : at + CF] = upacc[row_tap, rows : rows + CF, lanes : lanes + LANES]
    grad_ref[MIX_ROW : MIX_ROW + 192] = mixacc[:, :LANES]
    grad_ref[MIX_ROW + 192 : HEAD_ROW] = jnp.concatenate(
        [mixacc[:, LANES:], jnp.zeros((192, CF), F32)], axis=1
    )
    grad_ref[HEAD_ROW : HEAD_ROW + COUT] = jnp.concatenate(
        [head_sum, jnp.zeros((COUT, CF), F32)], axis=1
    )
    grad_ref[HEAD_ROW + COUT :] = jnp.zeros((GRAD_ROWS - HEAD_ROW - COUT, LANES), F32)
    for copy in copies:
        copy.wait_send()


def stages_of(nf, npat):
    nz = min(4, max(1, npat // 2))
    nx = npat // (2 * nz)
    return nz, nx


def sum_kernel(nf, npat, grad_ref, up_ref, mix_ref, headg_ref, total, final, one, two, three, send_sem, recv_sem):
    nz, nx = stages_of(nf, npat)
    me_f, me_p = lax.axis_index("face"), lax.axis_index("patch")
    core = lax.rem(me_p, 2)
    z = lax.rem(me_p // 2, nz)
    x = me_p // (2 * nz)

    def core_peer(k):
        return (me_f, me_p - core + lax.rem(core + k, 2))

    def x_peer(k):
        return (me_f, lax.rem(x + k, nx) * 2 * nz + z * 2 + core)

    def zy_peer(k):
        kz, kf = k % nz, k // nz
        return (lax.rem(me_f + kf, nf), x * 2 * nz + lax.rem(z + kz, nz) * 2 + core)

    nzy = nz * nf
    half = GRAD_ROWS // 2
    quarter = half // nx
    piece = quarter // nzy
    groups = ((core_peer, 2), (x_peer, nx), (zy_peer, nzy))

    barrier = pltpu.get_barrier_semaphore()
    count = 0
    for peer, size in groups:
        for k in range(1, size):
            pl.semaphore_signal(barrier, inc=1, device_id=peer(k), device_id_type=MESH)
            count += 1
    pl.semaphore_wait(barrier, count)

    sems = [0]
    pending = []

    def send(source, target, device):
        number = sems[0]
        sems[0] += 1
        copy = pltpu.make_async_remote_copy(
            src_ref=source, dst_ref=target,
            send_sem=send_sem.at[number], recv_sem=recv_sem.at[number],
            device_id=device, device_id_type=MESH,
        )
        copy.start()
        pending.append(copy)
        return copy

    def rows(start, size):
        return pl.ds(pl.multiple_of(start, 8), size)

    def index_core(k):
        return lax.rem(core + k, 2)

    def index_x(k):
        return lax.rem(x + k, nx)

    def index_zy(k):
        return lax.rem(me_f + k // nz, nf) * nz + lax.rem(z + k % nz, nz)

    copy = send(grad_ref.at[rows(index_core(1) * half, half)], one.at[0], core_peer(1))
    copy.wait_recv()
    base = index_core(0) * half
    total[rows(base, half)] = grad_ref[rows(base, half)] + one[0]
    arrivals = [
        send(total.at[rows(base + index_x(k) * quarter, quarter)], two.at[k - 1], x_peer(k))
        for k in range(1, nx)
    ]
    base_x = base + index_x(0) * quarter
    value = total[rows(base_x, quarter)]
    for k, copy in enumerate(arrivals):
        copy.wait_recv()
        value = value + two[k]
    total[rows(base_x, quarter)] = value
    arrivals = [
        send(total.at[rows(base_x + index_zy(k) * piece, piece)], three.at[k - 1], zy_peer(k))
        for k in range(1, nzy)
    ]
    base_zy = base_x + index_zy(0) * piece
    value = total[rows(base_zy, piece)]
    for k, copy in enumerate(arrivals):
        copy.wait_recv()
        value = value + three[k]
    final[rows(base_zy, piece)] = value

    def share(start, size, peer, count):
        region = final.at[rows(start, size)]
        started = [send(region, region, peer(k)) for k in range(1, count)]
        for copy in started:
            copy.wait_recv()

    share(base_zy, piece, zy_peer, nzy)
    share(base_x, quarter, x_peer, nx)
    share(base, half, core_peer, 2)

    up_ref[...] = final[:MIX_ROW]
    for col_tap in range(3):
        for row_tap in range(3):
            at = MIX_ROW + (col_tap // 2) * 192 + row_tap * CF
            lanes = (col_tap % 2) * CF
            to = (col_tap * 3 + row_tap) * CF
            mix_ref[to : to + CF] = final[at : at + CF, lanes : lanes + CF]
    headg_ref[...] = final[HEAD_ROW : HEAD_ROW + COUT, :CF]
    for copy in pending:
        copy.wait_send()


def vmem(count):
    return [pl.BlockSpec(memory_space=pltpu.VMEM)] * count


def per_device(nf, npat, coarse, w_up, w_mix, w_head, send_index, slot_ids, fractions, head_cot):
    by_column = coarse.transpose(1, 0, 2)
    edge = jnp.concatenate(
        [coarse[:, :, 0], coarse[:, :, -1], jnp.zeros((CIN, LANES - 2 * COLS), BF16)], axis=1
    )
    mixing = w_mix.transpose(1, 2, 0, 3).reshape(3 * CF, 3 * CF)
    back = mixing.T
    start = send_index[0, 2, 0:1] // 256
    points = slot_ids.shape[1]
    run = COLS * COUT
    scratch = [
        pltpu.VMEM((COLS + 3, CIN, LANES), BF16),
        pltpu.VMEM((COLS + 2, CIN, LANES), BF16),
        pltpu.VMEM((len(NEIGHBOURS), CIN, LANES), BF16),
        pltpu.VMEM((6 * CF, 2 * CIN), BF16),
        pltpu.VMEM((36, CF, 256), BF16),
        pltpu.VMEM((36, CF, 256), F32),
        pltpu.VMEM((32, CF, 256), F32),
        pltpu.VMEM((32, CF, 256), BF16),
        pltpu.VMEM((32, COUT, 256), F32),
        pltpu.VMEM((16, 16, 256), BF16),
        pltpu.VMEM((32, 16, 256), BF16),
        pltpu.VMEM((4 * run, 256), F32),
        pltpu.VMEM((3, run, 256), F32),
        pltpu.VMEM((48, COUT, 256), F32),
        pltpu.VMEM((34, CF, 256), BF16),
        pltpu.VMEM((CF, LANES), F32),
        pltpu.VMEM((len(ROW_NEIGHBOURS) + 1, CF, LANES), BF16),
        pltpu.VMEM((34, 3 * CF, 256), F32),
        pltpu.VMEM((8, LANES), F32),
        pltpu.VMEM((3 * CF, 3 * CF), F32),
        pltpu.VMEM((3, 2 * CF, 2 * CIN), F32),
        pltpu.SemaphoreType.DMA((24,)),
        pltpu.SemaphoreType.DMA((24,)),
    ]
    head, grads = pl.pallas_call(
        functools.partial(local_kernel, nf, npat),
        out_shape=(
            jax.ShapeDtypeStruct((COUT, points), F32),
            jax.ShapeDtypeStruct((GRAD_ROWS, LANES), F32),
        ),
        in_specs=[pl.BlockSpec(memory_space=pltpu.SMEM)] + vmem(10),
        out_specs=tuple(vmem(2)),
        scratch_shapes=scratch,
        compiler_params=pltpu.CompilerParams(
            collective_id=0, has_side_effects=True, vmem_limit_bytes=56 * 2**20
        ),
        name="local",
    )(start, by_column, edge, w_up, mixing, back, w_head, w_head.T, slot_ids, fractions, head_cot)

    nz, nx = stages_of(nf, npat)
    nzy = nz * nf
    half = GRAD_ROWS // 2
    quarter = half // nx
    piece = quarter // nzy
    sends = 2 * (1 + nx - 1 + nzy - 1)
    up, mix, head_grad = pl.pallas_call(
        functools.partial(sum_kernel, nf, npat),
        out_shape=(
            jax.ShapeDtypeStruct((9 * CF, CIN), F32),
            jax.ShapeDtypeStruct((9 * CF, CF), F32),
            jax.ShapeDtypeStruct((COUT, CF), F32),
        ),
        in_specs=vmem(1),
        out_specs=tuple(vmem(3)),
        scratch_shapes=[
            pltpu.VMEM((GRAD_ROWS, LANES), F32),
            pltpu.VMEM((GRAD_ROWS, LANES), F32),
            pltpu.VMEM((1, half, LANES), F32),
            pltpu.VMEM((max(1, nx - 1), quarter, LANES), F32),
            pltpu.VMEM((nzy - 1, piece, LANES), F32),
            pltpu.SemaphoreType.DMA((sends,)),
            pltpu.SemaphoreType.DMA((sends,)),
        ],
        compiler_params=pltpu.CompilerParams(
            collective_id=1, has_side_effects=True, vmem_limit_bytes=32 * 2**20
        ),
        name="sum",
    )(grads)
    return head, up.reshape(3, 3, CF, CIN), mix.reshape(3, 3, CF, CF), head_grad


def solution(mesh):
    placed = (
        P(None, "patch", "face"),
        P(),
        P(),
        P(),
        P("face", "patch", None),
        P(None, ("face", "patch")),
        P(None, ("face", "patch")),
        P(None, ("face", "patch")),
    )
    return jax.shard_map(
        functools.partial(per_device, mesh.shape["face"], mesh.shape["patch"]),
        mesh=mesh,
        in_specs=placed,
        out_specs=(P(None, ("face", "patch")), P(), P(), P()),
        check_vma=False,
    )
```

```python
import functools

import jax
import jax.numpy as jnp
from jax import lax
from jax.experimental import pallas as pl
from jax.experimental.pallas import tpu as pltpu
from jax.sharding import PartitionSpec as P

MESH = pl.DeviceIdType.MESH
F32 = jnp.float32
BF16 = jnp.bfloat16

LANES = 128
CIN = 128
CF = 64
COUT = 8
COLS = 16
POINT_TILE = 2048
GRAD_ROWS = 1024
MIX_ROW = 9 * CF
HEAD_ROW = MIX_ROW + 6 * CF
NEIGHBOURS = tuple((df, dp) for df in (-1, 0, 1) for dp in (-1, 0, 1) if (df, dp) != (0, 0))
ROW_NEIGHBOURS = tuple(pair for pair in NEIGHBOURS if pair[0] != 0)


def dot(left, right):
    return lax.dot_general(left, right, (((1,), (0,)), ((), ())), preferred_element_type=F32)


def dot_nt(left, right):
    return lax.dot_general(left, right, (((1,), (1,)), ((), ())), preferred_element_type=F32)


def turn(value, steps):
    if isinstance(steps, int):
        steps = steps % LANES
        if steps == 0:
            return value
    return pltpu.roll(value, steps, axis=1)


def sigmoid(value):
    return 0.5 * jnp.tanh(0.5 * value) + 0.5


def row_weights(slot, along):
    width = slot.shape[1]
    larger = jnp.maximum(along, 1.0 - along)
    upper, lower = along / larger, (1.0 - along) / larger
    place = lax.broadcasted_iota(jnp.int32, (256, width), 0)
    natural = 2 * (place & 127) + (place >> 7)
    away = natural - (slot & 255)
    weight = jnp.where(away == 0, lower, jnp.where(away == 1, upper, 0.0))
    return weight.astype(BF16), larger


def local_kernel(
    nf, npat,
    send_ref, coarse_ref, wup_ref, wmix_ref, whead_ref,
    slot_ref, frac_ref, cot_ref,
    head_ref, grad_ref,
    ext, exts, edges, upw, mixw, backw, hid, slope1, slope2, feat, gown, gsend, table,
    sacc, srecv, pad, sc, strip, strips, zbuf, mixacc, upacc, starts, start_sem,
    send_sem, recv_sem,
):
    me_f, me_p = lax.axis_index("face"), lax.axis_index("patch")

    def device(df, dp):
        return (lax.rem(me_f + df + nf, nf), lax.rem(me_p + dp + npat, npat))

    start_copy = pltpu.make_async_copy(send_ref.at[0, :, pl.ds(0, LANES)], starts, start_sem)
    start_copy.start()
    barrier = pltpu.get_barrier_semaphore()
    partners = NEIGHBOURS + ((0, 2), (0, -2))
    for df, dp in partners:
        pl.semaphore_signal(barrier, inc=1, device_id=device(df, dp), device_id_type=MESH)
    pl.semaphore_wait(barrier, len(partners))

    copies = []

    def send(source, target, offset):
        number = len(copies)
        copy = pltpu.make_async_remote_copy(
            src_ref=source, dst_ref=target,
            send_sem=send_sem.at[number], recv_sem=recv_sem.at[number],
            device_id=device(*offset), device_id_type=MESH,
        )
        copy.start()
        copies.append(copy)
        return copy

    lane = lax.broadcasted_iota(jnp.int32, (CIN, LANES), 1)
    lane64 = lane[:CF]
    edge = jnp.zeros((CIN, LANES), F32)
    for j in range(COLS):
        column = coarse_ref[j].astype(F32)
        edge = jnp.where(lane == j, turn(column, j), edge)
        edge = jnp.where(lane == COLS + j, turn(column, COLS + 1 + j), edge)
    edge_own = edges.at[len(NEIGHBOURS)]
    edge_own[...] = edge.astype(BF16)
    coarse_copies = [
        send(coarse_ref.at[0], ext.at[COLS + 1], (0, -1)),
        send(coarse_ref.at[COLS - 1], ext.at[0], (0, 1)),
    ]
    for number, offset in enumerate(NEIGHBOURS):
        coarse_copies.append(send(edge_own, edges.at[number], offset))

    ext[1 : COLS + 1] = coarse_ref[...]
    ext[COLS + 2] = jnp.zeros((CIN, LANES), BF16)
    for row_tap in range(3):
        low = slice(row_tap * CF, (row_tap + 1) * CF)
        high = slice((3 + row_tap) * CF, (4 + row_tap) * CF)
        upw[low, :CIN] = wup_ref[1, row_tap]
        upw[low, CIN:] = jnp.zeros((CF, CIN), BF16)
        upw[high, :CIN] = wup_ref[2, row_tap]
        upw[high, CIN:] = wup_ref[0, row_tap]
    mix_rows = [
        jnp.concatenate([wmix_ref[col_tap, row_tap].astype(F32) for col_tap in range(3)], axis=1)
        for row_tap in range(3)
    ]
    mixing = jnp.concatenate(mix_rows, axis=0)
    mixw[...] = mixing.astype(BF16)
    backw[...] = mixing.T.astype(BF16)

    sacc[...] = jnp.zeros_like(sacc)

    @pl.loop(0, slot_ref.shape[1] // POINT_TILE)
    def _(step):
        here = pl.ds(pl.multiple_of(step * POINT_TILE, POINT_TILE), POINT_TILE)
        slot = slot_ref[0:1, here]
        along, across = frac_ref[0:1, here], frac_ref[1:2, here]
        rows, larger = row_weights(slot, along)
        cot = cot_ref[:, here] * larger
        near, far = cot * (1.0 - across), cot * across
        column = jnp.broadcast_to(slot >> 8, near.shape)[None]
        number = lax.broadcasted_iota(jnp.int32, (64,) + near.shape, 0)
        away = number - column
        terms = jnp.where(away == 0, near[None], jnp.where(away == 1, far[None], 0.0))
        sacc[...] += dot_nt(terms.reshape(64 * COUT, POINT_TILE).astype(BF16), rows)

    run = COLS * COUT
    pad[0:16] = jnp.zeros((16, COUT, 256), F32)
    pad[16:32] = sacc[2 * run : 3 * run].reshape(16, COUT, 256)
    pad[32:48] = jnp.zeros((16, COUT, 256), F32)
    back_copies = [
        send(sacc.at[0:run], srecv.at[0], (0, 2)),
        send(sacc.at[run : 2 * run], srecv.at[1], (0, 1)),
        send(sacc.at[3 * run : 4 * run], srecv.at[2], (0, -1)),
    ]

    for copy in coarse_copies:
        copy.wait_recv()
    above = jnp.where(me_f > 0, 1.0, 0.0).astype(F32)
    below = jnp.where(me_f < nf - 1, 1.0, 0.0).astype(F32)

    def arrived(buffer, df, dp):
        pairs = NEIGHBOURS if buffer is edges else ROW_NEIGHBOURS
        return buffer[pairs.index((-df, -dp))].astype(F32)

    def between(low, high, index):
        return jnp.logical_and(index >= low, index < high)

    top = jnp.where(between(1, 17, lane), turn(arrived(edges, -1, 0), -15), 0.0)
    top = jnp.where(lane == 0, turn(arrived(edges, -1, -1), -31), top)
    top = jnp.where(lane == 17, turn(arrived(edges, -1, 1), 1), top) * above
    first_row = jnp.where(between(33, 49, lane), turn(edge, 33), 0.0)
    first_row = jnp.where(lane == 32, turn(arrived(edges, 0, -1), 17), first_row)
    first_row = jnp.where(lane == 49, turn(arrived(edges, 0, 1), 49), first_row)
    bottom = jnp.where(between(65, 81, lane), turn(arrived(edges, 1, 0), 65), 0.0)
    bottom = jnp.where(lane == 64, turn(arrived(edges, 1, -1), 49), bottom)
    bottom = jnp.where(lane == 81, turn(arrived(edges, 1, 1), 81), bottom) * below
    rim = top + first_row + bottom
    rim_pair = jnp.concatenate([rim, turn(rim, -1)], axis=0).astype(BF16)
    rim_out = dot(upw[...], rim_pair)
    rim_hidden = []
    for parity in range(2):
        part = rim_out[parity * 192 : (parity + 1) * 192]
        upper = part[128:192] + turn(part[0:64], -32)
        value = jnp.where(lane64 < 32, upper * above, jnp.where(between(64, 96, lane64), part[64:128], 0.0))
        rim_hidden.append(value * sigmoid(value))
    even_rim, odd_rim = rim_hidden
    mix_rim = [
        dot(mixw[...], jnp.concatenate([turn(odd_rim, 1), even_rim, odd_rim], axis=0).astype(BF16)),
        dot(mixw[...], jnp.concatenate([even_rim, odd_rim, turn(even_rim, -1)], axis=0).astype(BF16)),
    ]

    @pl.loop(0, 9, unroll=9)
    def _(step):
        t = 2 * step
        pair = [ext[pl.ds(t + k, 2)].reshape(2 * CIN, LANES) for k in range(2)]
        out = dot(upw[...], jnp.concatenate(pair, axis=1))
        for k in range(2):
            here = t + k
            for parity in range(2):
                part = out[parity * 192 : (parity + 1) * 192, k * LANES : (k + 1) * LANES]
                entering = turn(rim_out[parity * 192 : parity * 192 + 64], 63 - here)
                odd = part[128:192] + jnp.where(lane64 == 127, entering, turn(part[0:64], -1))
                value = jnp.concatenate([part[64:128], odd], axis=1)
                sigma = sigmoid(value)
                hid[2 * here + parity] = (value * sigma).astype(BF16)
                slope1[2 * here + parity] = sigma * (1.0 + value * (1.0 - sigma))
            shifted = turn(ext[here].astype(F32), -1)
            exts[here] = jnp.where(lane == 127, turn(rim, 63 - here), shifted).astype(BF16)

    weight = whead_ref[...]
    weight_high = weight.astype(BF16).astype(F32)
    head_pair = jnp.concatenate([weight_high, weight - weight_high], axis=0).astype(BF16)

    def mix_step(j):
        values = []
        for parity in range(2):
            q = 2 * j + parity
            out = dot(mixw[...], hid[pl.ds(q + 1, 3)].reshape(192, 256))
            low, mid, high = out[0:64], out[64:128], out[128:192]
            first = turn(mix_rim[parity][0:64], 127 - j)
            last = turn(mix_rim[parity][128:192], 62 - j)
            even = jnp.where(lane64 == 0, first, turn(low[:, LANES:], 1)) + mid[:, :LANES] + high[:, LANES:]
            odd = low[:, :LANES] + mid[:, LANES:] + jnp.where(lane64 == 127, last, turn(high[:, :LANES], -1))
            value = jnp.concatenate([even, odd], axis=1)
            sigma = sigmoid(value)
            feature = (value * sigma).astype(BF16)
            feat[q] = feature
            slope2[q] = sigma * (1.0 + value * (1.0 - sigma))
            both = dot(head_pair, feature)
            point_value = both[0:8] + both[8:16]
            gown[q] = point_value
            values.append(point_value)
        gsend[j] = jnp.concatenate(values, axis=0).astype(BF16)

    pl.loop(0, 8, unroll=8)(mix_step)
    value_copies = [
        send(gsend.at[0:8], table.at[0:8], (0, -2)),
        send(gsend.at[0:8], table.at[8:16], (0, -1)),
    ]
    pl.loop(8, 16, unroll=8)(mix_step)
    value_copies.append(send(gsend.at[8:16], table.at[24:32], (0, 1)))

    start_copy.wait()
    start = starts[2, 0] // 256
    for k in range(8):
        pair = [gown[start + 2 * k], gown[start + 2 * k + 1]]
        table[16 + k] = jnp.concatenate(pair, axis=0).astype(BF16)

    for copy in back_copies:
        copy.wait_recv()
    weight_t = whead_ref[...].T
    high_t = weight_t.astype(BF16).astype(F32)
    weight_three = jnp.concatenate([high_t, weight_t - high_t, high_t], axis=1).astype(BF16)
    strip[...] = jnp.zeros_like(strip)

    def cot_step(q, total, head_sum):
        high = total.astype(BF16).astype(F32)
        low = total - high
        fine = dot(weight_three, jnp.concatenate([high, high, low], axis=0).astype(BF16))
        value = fine * slope2[q]
        sc[q + 1] = value.astype(BF16)
        kept = jnp.where(lane64 == q, turn(value[:, :LANES], q), strip[...])
        strip[...] = jnp.where(lane64 == q + 32, turn(value[:, LANES:], q + 33), kept)
        both = dot_nt(jnp.concatenate([high, low], axis=0).astype(BF16), feat[q])
        return head_sum + both[0:8] + both[8:16]

    def row_of(number, q):
        return srecv[number, pl.ds(pl.multiple_of(q * COUT, COUT), COUT), :]

    def cot_low(q, head_sum):
        total = row_of(0, q) + row_of(1, q) + pad[16 + q - start]
        return cot_step(q, total, head_sum)

    def cot_high(q, head_sum):
        total = row_of(2, q - 16) + pad[16 + q - start]
        return cot_step(q, total, head_sum)

    head_sum = lax.fori_loop(0, 16, cot_low, jnp.zeros((COUT, CF), F32), unroll=8)
    head_sum = lax.fori_loop(16, 32, cot_high, head_sum, unroll=8)
    strips_own = strips.at[len(ROW_NEIGHBOURS)]
    strips_own[...] = strip[...].astype(BF16)
    cot_copies = [
        send(sc.at[1], sc.at[33], (0, -1)),
        send(sc.at[32], sc.at[0], (0, 1)),
    ]
    for number, offset in enumerate(ROW_NEIGHBOURS):
        cot_copies.append(send(strips_own, strips.at[number], offset))

    for copy in value_copies:
        copy.wait_recv()

    @pl.loop(0, slot_ref.shape[1] // POINT_TILE)
    def _(step):
        here = pl.ds(pl.multiple_of(step * POINT_TILE, POINT_TILE), POINT_TILE)
        slot = slot_ref[0:1, here]
        along, across = frac_ref[0:1, here], frac_ref[1:2, here]
        rows, larger = row_weights(slot, along)
        columns = dot(table[...].reshape(64 * COUT, 256), rows).reshape(64, COUT, POINT_TILE)
        column = jnp.broadcast_to(slot >> 8, (COUT, POINT_TILE))[None]
        number = lax.broadcasted_iota(jnp.int32, (64, COUT, POINT_TILE), 0)
        away = number - column
        near = jnp.broadcast_to((1.0 - across) * larger, (COUT, POINT_TILE))[None]
        far = jnp.broadcast_to(across * larger, (COUT, POINT_TILE))[None]
        weights = jnp.where(away == 0, near, jnp.where(away == 1, far, 0.0))
        head_ref[:, here] = jnp.sum(weights * columns, axis=0)

    for copy in cot_copies:
        copy.wait_recv()
    upper = jnp.where(between(1, 33, lane64), turn(arrived(strips, -1, 0), -31), 0.0)
    upper = jnp.where(lane64 == 0, turn(arrived(strips, -1, -1), -63), upper)
    upper = jnp.where(lane64 == 33, turn(arrived(strips, -1, 1), 1), upper) * above
    lower = jnp.where(between(65, 97, lane64), turn(arrived(strips, 1, 0), 65), 0.0)
    lower = jnp.where(lane64 == 64, turn(arrived(strips, 1, -1), 33), lower)
    lower = jnp.where(lane64 == 97, turn(arrived(strips, 1, 1), 97), lower) * below
    cot_rim = upper + lower

    def back_step(w):
        value = sc[w].astype(F32)
        even, odd = value[:, :LANES], value[:, LANES:]
        last = jnp.where(lane64 == 127, turn(cot_rim, 63 - w), turn(even, -1))
        first = jnp.where(lane64 == 0, turn(cot_rim, LANES - w), turn(odd, 1))
        taps = jnp.concatenate(
            [jnp.concatenate([odd, last], axis=1), value, jnp.concatenate([first, even], axis=1)],
            axis=0,
        ).astype(BF16)
        zbuf[w] = dot(backw[...], taps)
        return taps

    mixacc[...] = jnp.zeros_like(mixacc)
    back_step(0)

    @pl.loop(1, 33, unroll=8)
    def _(w):
        taps = back_step(w)
        mixacc[...] += dot_nt(taps, hid[pl.ds(w, 3)].reshape(192, 256))

    back_step(33)

    upacc[...] = jnp.zeros_like(upacc)

    @pl.loop(0, 8, unroll=8)
    def _(step):
        evens, odds = [], []
        for k in range(2):
            even_parts, odd_parts = [], []
            for parity in range(2):
                q = 4 * step + 2 * k + parity
                total = zbuf[q + 2, 0:64] + zbuf[q + 1, 64:128] + zbuf[q, 128:192]
                value = (total * slope1[q + 2]).astype(BF16)
                even_parts.append(value[:, :LANES])
                odd_parts.append(value[:, LANES:])
            evens.append(jnp.concatenate(even_parts, axis=0))
            odds.append(jnp.concatenate(odd_parts, axis=0))
        even = jnp.concatenate(evens, axis=1)
        odd = jnp.concatenate(odds, axis=1)

        def window(buffer):
            pair = [buffer[pl.ds(2 * step + 1 + k, 2)].reshape(2 * CIN, LANES) for k in range(2)]
            return jnp.concatenate(pair, axis=1)

        plain, moved = window(ext), window(exts)
        upacc[0] += dot_nt(odd, moved)
        upacc[1] += dot_nt(even, plain)
        upacc[2] += dot_nt(odd, plain)

    for row_tap in range(3):
        for col_tap, rows, lanes in ((0, 64, 128), (1, 0, 0), (2, 64, 0)):
            at = (col_tap * 3 + row_tap) * CF
            grad_ref[at : at + CF] = upacc[row_tap, rows : rows + CF, lanes : lanes + LANES]
    grad_ref[MIX_ROW : MIX_ROW + 192] = mixacc[:, :LANES]
    grad_ref[MIX_ROW + 192 : HEAD_ROW] = jnp.concatenate(
        [mixacc[:, LANES:], jnp.zeros((192, CF), F32)], axis=1
    )
    grad_ref[HEAD_ROW : HEAD_ROW + COUT] = jnp.concatenate(
        [head_sum, jnp.zeros((COUT, CF), F32)], axis=1
    )
    grad_ref[HEAD_ROW + COUT :] = jnp.zeros((GRAD_ROWS - HEAD_ROW - COUT, LANES), F32)
    for copy in copies:
        copy.wait_send()


def stages_of(nf, npat):
    nz = min(4, max(1, npat // 2))
    nx = npat // (2 * nz)
    return nz, nx


def sum_kernel(nf, npat, grad_ref, up_ref, mix_ref, headg_ref, total, final, one, two, three, send_sem, recv_sem):
    nz, nx = stages_of(nf, npat)
    me_f, me_p = lax.axis_index("face"), lax.axis_index("patch")
    core = lax.rem(me_p, 2)
    z = lax.rem(me_p // 2, nz)
    x = me_p // (2 * nz)

    def core_peer(k):
        return (me_f, me_p - core + lax.rem(core + k, 2))

    def x_peer(k):
        return (me_f, lax.rem(x + k, nx) * 2 * nz + z * 2 + core)

    def zy_peer(k):
        kz, kf = k % nz, k // nz
        return (lax.rem(me_f + kf, nf), x * 2 * nz + lax.rem(z + kz, nz) * 2 + core)

    nzy = nz * nf
    half = GRAD_ROWS // 2
    quarter = half // nx
    piece = quarter // nzy
    groups = ((core_peer, 2), (x_peer, nx), (zy_peer, nzy))

    barrier = pltpu.get_barrier_semaphore()
    count = 0
    for peer, size in groups:
        for k in range(1, size):
            pl.semaphore_signal(barrier, inc=1, device_id=peer(k), device_id_type=MESH)
            count += 1
    pl.semaphore_wait(barrier, count)

    sems = [0]
    pending = []

    def send(source, target, device):
        number = sems[0]
        sems[0] += 1
        copy = pltpu.make_async_remote_copy(
            src_ref=source, dst_ref=target,
            send_sem=send_sem.at[number], recv_sem=recv_sem.at[number],
            device_id=device, device_id_type=MESH,
        )
        copy.start()
        pending.append(copy)
        return copy

    def rows(start, size):
        return pl.ds(pl.multiple_of(start, 8), size)

    def index_core(k):
        return lax.rem(core + k, 2)

    def index_x(k):
        return lax.rem(x + k, nx)

    def index_zy(k):
        return lax.rem(me_f + k // nz, nf) * nz + lax.rem(z + k % nz, nz)

    copy = send(grad_ref.at[rows(index_core(1) * half, half)], one.at[0], core_peer(1))
    copy.wait_recv()
    base = index_core(0) * half
    total[rows(base, half)] = grad_ref[rows(base, half)] + one[0]
    arrivals = [
        send(total.at[rows(base + index_x(k) * quarter, quarter)], two.at[k - 1], x_peer(k))
        for k in range(1, nx)
    ]
    base_x = base + index_x(0) * quarter
    value = total[rows(base_x, quarter)]
    for k, copy in enumerate(arrivals):
        copy.wait_recv()
        value = value + two[k]
    total[rows(base_x, quarter)] = value
    arrivals = [
        send(total.at[rows(base_x + index_zy(k) * piece, piece)], three.at[k - 1], zy_peer(k))
        for k in range(1, nzy)
    ]
    base_zy = base_x + index_zy(0) * piece
    value = total[rows(base_zy, piece)]
    for k, copy in enumerate(arrivals):
        copy.wait_recv()
        value = value + three[k]
    final[rows(base_zy, piece)] = value

    def share(start, size, peer, count):
        region = final.at[rows(start, size)]
        started = [send(region, region, peer(k)) for k in range(1, count)]
        for copy in started:
            copy.wait_recv()

    share(base_zy, piece, zy_peer, nzy)
    share(base_x, quarter, x_peer, nx)
    share(base, half, core_peer, 2)

    up_ref[...] = final[:MIX_ROW]
    for col_tap in range(3):
        for row_tap in range(3):
            at = MIX_ROW + (col_tap // 2) * 192 + row_tap * CF
            lanes = (col_tap % 2) * CF
            to = (col_tap * 3 + row_tap) * CF
            mix_ref[to : to + CF] = final[at : at + CF, lanes : lanes + CF]
    headg_ref[...] = final[HEAD_ROW : HEAD_ROW + COUT, :CF]
    for copy in pending:
        copy.wait_send()


def vmem(count):
    return [pl.BlockSpec(memory_space=pltpu.VMEM)] * count


def per_device(nf, npat, coarse, w_up, w_mix, w_head, send_index, slot_ids, fractions, head_cot):
    by_column = coarse.transpose(1, 0, 2)
    points = slot_ids.shape[1]
    run = COLS * COUT
    scratch = [
        pltpu.VMEM((COLS + 3, CIN, LANES), BF16),
        pltpu.VMEM((COLS + 2, CIN, LANES), BF16),
        pltpu.VMEM((len(NEIGHBOURS) + 1, CIN, LANES), BF16),
        pltpu.VMEM((6 * CF, 2 * CIN), BF16),
        pltpu.VMEM((3 * CF, 3 * CF), BF16),
        pltpu.VMEM((3 * CF, 3 * CF), BF16),
        pltpu.VMEM((36, CF, 256), BF16),
        pltpu.VMEM((36, CF, 256), F32),
        pltpu.VMEM((32, CF, 256), F32),
        pltpu.VMEM((32, CF, 256), BF16),
        pltpu.VMEM((32, COUT, 256), F32),
        pltpu.VMEM((16, 16, 256), BF16),
        pltpu.VMEM((32, 16, 256), BF16),
        pltpu.VMEM((4 * run, 256), F32),
        pltpu.VMEM((3, run, 256), F32),
        pltpu.VMEM((48, COUT, 256), F32),
        pltpu.VMEM((34, CF, 256), BF16),
        pltpu.VMEM((CF, LANES), F32),
        pltpu.VMEM((len(ROW_NEIGHBOURS) + 1, CF, LANES), BF16),
        pltpu.VMEM((34, 3 * CF, 256), F32),
        pltpu.VMEM((3 * CF, 3 * CF), F32),
        pltpu.VMEM((3, 2 * CF, 2 * CIN), F32),
        pltpu.SMEM((4, LANES), jnp.int32),
        pltpu.SemaphoreType.DMA,
        pltpu.SemaphoreType.DMA((24,)),
        pltpu.SemaphoreType.DMA((24,)),
    ]
    head, grads = pl.pallas_call(
        functools.partial(local_kernel, nf, npat),
        out_shape=(
            jax.ShapeDtypeStruct((COUT, points), F32),
            jax.ShapeDtypeStruct((GRAD_ROWS, LANES), F32),
        ),
        in_specs=[pl.BlockSpec(memory_space=pl.ANY)] + vmem(7),
        out_specs=tuple(vmem(2)),
        scratch_shapes=scratch,
        compiler_params=pltpu.CompilerParams(
            collective_id=0, has_side_effects=True, vmem_limit_bytes=56 * 2**20
        ),
        name="local",
    )(send_index, by_column, w_up, w_mix, w_head, slot_ids, fractions, head_cot)

    nz, nx = stages_of(nf, npat)
    nzy = nz * nf
    half = GRAD_ROWS // 2
    quarter = half // nx
    piece = quarter // nzy
    sends = 2 * (1 + nx - 1 + nzy - 1)
    up, mix, head_grad = pl.pallas_call(
        functools.partial(sum_kernel, nf, npat),
        out_shape=(
            jax.ShapeDtypeStruct((9 * CF, CIN), F32),
            jax.ShapeDtypeStruct((9 * CF, CF), F32),
            jax.ShapeDtypeStruct((COUT, CF), F32),
        ),
        in_specs=vmem(1),
        out_specs=tuple(vmem(3)),
        scratch_shapes=[
            pltpu.VMEM((GRAD_ROWS, LANES), F32),
            pltpu.VMEM((GRAD_ROWS, LANES), F32),
            pltpu.VMEM((1, half, LANES), F32),
            pltpu.VMEM((max(1, nx - 1), quarter, LANES), F32),
            pltpu.VMEM((nzy - 1, piece, LANES), F32),
            pltpu.SemaphoreType.DMA((sends,)),
            pltpu.SemaphoreType.DMA((sends,)),
        ],
        compiler_params=pltpu.CompilerParams(
            collective_id=1, has_side_effects=True, vmem_limit_bytes=32 * 2**20
        ),
        name="sum",
    )(grads)
    return head, up.reshape(3, 3, CF, CIN), mix.reshape(3, 3, CF, CF), head_grad


def solution(mesh):
    placed = (
        P(None, "patch", "face"),
        P(),
        P(),
        P(),
        P("face", "patch", None),
        P(None, ("face", "patch")),
        P(None, ("face", "patch")),
        P(None, ("face", "patch")),
    )
    return jax.shard_map(
        functools.partial(per_device, mesh.shape["face"], mesh.shape["patch"]),
        mesh=mesh,
        in_specs=placed,
        out_specs=(P(None, ("face", "patch")), P(), P(), P()),
        check_vma=False,
    )
```

```python
import functools

import jax
import jax.numpy as jnp
from jax import lax
from jax.experimental import pallas as pl
from jax.experimental.pallas import tpu as pltpu
from jax.sharding import PartitionSpec as P

MESH = pl.DeviceIdType.MESH
F32 = jnp.float32
BF16 = jnp.bfloat16

LANES = 128
CIN = 128
CF = 64
COUT = 8
COLS = 16
POINT_TILE = 2048
SAMPLE_CUTS = (3, 5, 7)
GRAD_ROWS = 1024
MIX_ROW = 9 * CF
HEAD_ROW = MIX_ROW + 6 * CF
NEIGHBOURS = tuple((df, dp) for df in (-1, 0, 1) for dp in (-1, 0, 1) if (df, dp) != (0, 0))
ROW_NEIGHBOURS = tuple(pair for pair in NEIGHBOURS if pair[0] != 0)


def dot(left, right):
    return lax.dot_general(left, right, (((1,), (0,)), ((), ())), preferred_element_type=F32)


def dot_nt(left, right):
    return lax.dot_general(left, right, (((1,), (1,)), ((), ())), preferred_element_type=F32)


def turn(value, steps):
    if isinstance(steps, int):
        steps = steps % LANES
        if steps == 0:
            return value
    return pltpu.roll(value, steps, axis=1)


def sigmoid(value):
    return 0.5 * jnp.tanh(0.5 * value) + 0.5


def row_weights(slot, along):
    width = slot.shape[1]
    larger = jnp.maximum(along, 1.0 - along)
    upper, lower = along / larger, (1.0 - along) / larger
    place = lax.broadcasted_iota(jnp.int32, (256, width), 0)
    natural = 2 * (place & 127) + (place >> 7)
    away = natural - (slot & 255)
    weight = jnp.where(away == 0, lower, jnp.where(away == 1, upper, 0.0))
    return weight.astype(BF16), larger


def local_kernel(
    nf, npat,
    send_ref, coarse_ref, wup_ref, wmix_ref, whead_ref,
    slot_ref, frac_ref, cot_ref,
    head_ref, up_ref, mix_ref, headg_ref,
    ext, exts, edges, upw, mixw, backw, hid, slope1, slope2, feat, gown, gsend, table,
    sacc, srecv, pad, sc, strip, strips, zbuf, mixacc, upacc, starts, start_sem,
    grads, final, total, other, parts, sum_send, sum_recv,
    send_sem, recv_sem,
):
    me_f, me_p = lax.axis_index("face"), lax.axis_index("patch")

    def device(df, dp):
        return (lax.rem(me_f + df + nf, nf), lax.rem(me_p + dp + npat, npat))

    start_copy = pltpu.make_async_copy(send_ref.at[0, :, pl.ds(0, LANES)], starts, start_sem)
    start_copy.start()
    barrier = pltpu.get_barrier_semaphore()
    partners = NEIGHBOURS + ((0, 2), (0, -2))
    chips = nf * npat // 2
    core = lax.rem(me_p, 2)
    here_chip = me_f * (npat // 2) + me_p // 2
    core_peer = (me_f, me_p + 1 - 2 * core)

    def chip_at(k):
        face = lax.rem(me_f + k // (npat // 2), nf)
        pair = lax.rem(me_p // 2 + k % (npat // 2), npat // 2)
        return face * (npat // 2) + pair, (face, 2 * pair + core)

    for df, dp in partners:
        pl.semaphore_signal(barrier, inc=1, device_id=device(df, dp), device_id_type=MESH)
    pl.semaphore_signal(barrier, inc=1, device_id=core_peer, device_id_type=MESH)

    @pl.loop(1, chips)
    def _(k):
        pl.semaphore_signal(barrier, inc=1, device_id=chip_at(k)[1], device_id_type=MESH)

    pl.semaphore_wait(barrier, len(partners) + chips)

    copies = []

    def send(source, target, offset):
        number = len(copies)
        copy = pltpu.make_async_remote_copy(
            src_ref=source, dst_ref=target,
            send_sem=send_sem.at[number], recv_sem=recv_sem.at[number],
            device_id=device(*offset), device_id_type=MESH,
        )
        copy.start()
        copies.append(copy)
        return copy

    lane = lax.broadcasted_iota(jnp.int32, (CIN, LANES), 1)
    lane64 = lane[:CF]
    edge = jnp.zeros((CIN, LANES), F32)
    for j in range(COLS):
        column = coarse_ref[j].astype(F32)
        edge = jnp.where(lane == j, turn(column, j), edge)
        edge = jnp.where(lane == COLS + j, turn(column, COLS + 1 + j), edge)
    edge_own = edges.at[len(NEIGHBOURS)]
    edge_own[...] = edge.astype(BF16)
    coarse_copies = [
        send(coarse_ref.at[0], ext.at[COLS + 1], (0, -1)),
        send(coarse_ref.at[COLS - 1], ext.at[0], (0, 1)),
    ]
    for number, offset in enumerate(NEIGHBOURS):
        coarse_copies.append(send(edge_own, edges.at[number], offset))

    ext[1 : COLS + 1] = coarse_ref[...]
    ext[COLS + 2] = jnp.zeros((CIN, LANES), BF16)
    for row_tap in range(3):
        low = slice(row_tap * CF, (row_tap + 1) * CF)
        high = slice((3 + row_tap) * CF, (4 + row_tap) * CF)
        upw[low, :CIN] = wup_ref[1, row_tap]
        upw[low, CIN:] = jnp.zeros((CF, CIN), BF16)
        upw[high, :CIN] = wup_ref[2, row_tap]
        upw[high, CIN:] = wup_ref[0, row_tap]
    mix_rows = [
        jnp.concatenate([wmix_ref[col_tap, row_tap].astype(F32) for col_tap in range(3)], axis=1)
        for row_tap in range(3)
    ]
    mixing = jnp.concatenate(mix_rows, axis=0)
    mixw[...] = mixing.astype(BF16)
    backw[...] = mixing.T.astype(BF16)

    sacc[...] = jnp.zeros_like(sacc)

    @pl.loop(0, slot_ref.shape[1] // POINT_TILE)
    def _(step):
        here = pl.ds(pl.multiple_of(step * POINT_TILE, POINT_TILE), POINT_TILE)
        slot = slot_ref[0:1, here]
        along, across = frac_ref[0:1, here], frac_ref[1:2, here]
        rows, larger = row_weights(slot, along)
        cot = cot_ref[:, here] * larger
        near, far = cot * (1.0 - across), cot * across
        column = jnp.broadcast_to(slot >> 8, near.shape)[None]
        number = lax.broadcasted_iota(jnp.int32, (64,) + near.shape, 0)
        away = number - column
        terms = jnp.where(away == 0, near[None], jnp.where(away == 1, far[None], 0.0))
        sacc[...] += dot_nt(terms.reshape(64 * COUT, POINT_TILE).astype(BF16), rows)

    run = COLS * COUT
    pad[0:16] = jnp.zeros((16, COUT, 256), F32)
    pad[16:32] = sacc[2 * run : 3 * run].reshape(16, COUT, 256)
    pad[32:48] = jnp.zeros((16, COUT, 256), F32)
    back_copies = [
        send(sacc.at[0:run], srecv.at[0], (0, 2)),
        send(sacc.at[run : 2 * run], srecv.at[1], (0, 1)),
        send(sacc.at[3 * run : 4 * run], srecv.at[2], (0, -1)),
    ]

    for copy in coarse_copies:
        copy.wait_recv()
    above = jnp.where(me_f > 0, 1.0, 0.0).astype(F32)
    below = jnp.where(me_f < nf - 1, 1.0, 0.0).astype(F32)

    def arrived(buffer, df, dp):
        pairs = NEIGHBOURS if buffer is edges else ROW_NEIGHBOURS
        return buffer[pairs.index((-df, -dp))].astype(F32)

    def between(low, high, index):
        return jnp.logical_and(index >= low, index < high)

    top = jnp.where(between(1, 17, lane), turn(arrived(edges, -1, 0), -15), 0.0)
    top = jnp.where(lane == 0, turn(arrived(edges, -1, -1), -31), top)
    top = jnp.where(lane == 17, turn(arrived(edges, -1, 1), 1), top) * above
    first_row = jnp.where(between(33, 49, lane), turn(edge, 33), 0.0)
    first_row = jnp.where(lane == 32, turn(arrived(edges, 0, -1), 17), first_row)
    first_row = jnp.where(lane == 49, turn(arrived(edges, 0, 1), 49), first_row)
    bottom = jnp.where(between(65, 81, lane), turn(arrived(edges, 1, 0), 65), 0.0)
    bottom = jnp.where(lane == 64, turn(arrived(edges, 1, -1), 49), bottom)
    bottom = jnp.where(lane == 81, turn(arrived(edges, 1, 1), 81), bottom) * below
    rim = top + first_row + bottom
    rim_pair = jnp.concatenate([rim, turn(rim, -1)], axis=0).astype(BF16)
    rim_out = dot(upw[...], rim_pair)
    rim_hidden = []
    for parity in range(2):
        part = rim_out[parity * 192 : (parity + 1) * 192]
        upper = part[128:192] + turn(part[0:64], -32)
        value = jnp.where(lane64 < 32, upper * above, jnp.where(between(64, 96, lane64), part[64:128], 0.0))
        rim_hidden.append(value * sigmoid(value))
    even_rim, odd_rim = rim_hidden
    mix_rim = [
        dot(mixw[...], jnp.concatenate([turn(odd_rim, 1), even_rim, odd_rim], axis=0).astype(BF16)),
        dot(mixw[...], jnp.concatenate([even_rim, odd_rim, turn(even_rim, -1)], axis=0).astype(BF16)),
    ]

    @pl.loop(0, 9, unroll=9)
    def _(step):
        t = 2 * step
        pair = [ext[pl.ds(t + k, 2)].reshape(2 * CIN, LANES) for k in range(2)]
        out = dot(upw[...], jnp.concatenate(pair, axis=1))
        for k in range(2):
            here = t + k
            for parity in range(2):
                part = out[parity * 192 : (parity + 1) * 192, k * LANES : (k + 1) * LANES]
                entering = turn(rim_out[parity * 192 : parity * 192 + 64], 63 - here)
                odd = part[128:192] + jnp.where(lane64 == 127, entering, turn(part[0:64], -1))
                value = jnp.concatenate([part[64:128], odd], axis=1)
                sigma = sigmoid(value)
                hid[2 * here + parity] = (value * sigma).astype(BF16)
                slope1[2 * here + parity] = sigma * (1.0 + value * (1.0 - sigma))
            shifted = turn(ext[here].astype(F32), -1)
            exts[here] = jnp.where(lane == 127, turn(rim, 63 - here), shifted).astype(BF16)

    weight = whead_ref[...]
    weight_high = weight.astype(BF16).astype(F32)
    head_pair = jnp.concatenate([weight_high, weight - weight_high], axis=0).astype(BF16)

    def mix_step(j):
        values = []
        for parity in range(2):
            q = 2 * j + parity
            out = dot(mixw[...], hid[pl.ds(q + 1, 3)].reshape(192, 256))
            low, mid, high = out[0:64], out[64:128], out[128:192]
            first = turn(mix_rim[parity][0:64], 127 - j)
            last = turn(mix_rim[parity][128:192], 62 - j)
            even = jnp.where(lane64 == 0, first, turn(low[:, LANES:], 1)) + mid[:, :LANES] + high[:, LANES:]
            odd = low[:, :LANES] + mid[:, LANES:] + jnp.where(lane64 == 127, last, turn(high[:, :LANES], -1))
            value = jnp.concatenate([even, odd], axis=1)
            sigma = sigmoid(value)
            feature = (value * sigma).astype(BF16)
            feat[q] = feature
            slope2[q] = sigma * (1.0 + value * (1.0 - sigma))
            both = dot(head_pair, feature)
            point_value = both[0:8] + both[8:16]
            gown[q] = point_value
            values.append(point_value)
        gsend[j] = jnp.concatenate(values, axis=0).astype(BF16)

    pl.loop(0, 8, unroll=8)(mix_step)
    value_copies = [
        send(gsend.at[0:8], table.at[0:8], (0, -2)),
        send(gsend.at[0:8], table.at[8:16], (0, -1)),
    ]
    pl.loop(8, 16, unroll=8)(mix_step)
    value_copies.append(send(gsend.at[8:16], table.at[24:32], (0, 1)))

    start_copy.wait()
    start = starts[2, 0] // 256
    for k in range(8):
        pair = [gown[start + 2 * k], gown[start + 2 * k + 1]]
        table[16 + k] = jnp.concatenate(pair, axis=0).astype(BF16)

    for copy in back_copies:
        copy.wait_recv()
    weight_t = whead_ref[...].T
    high_t = weight_t.astype(BF16).astype(F32)
    weight_three = jnp.concatenate([high_t, weight_t - high_t, high_t], axis=1).astype(BF16)
    strip[...] = jnp.zeros_like(strip)

    def cot_step(q, total, head_sum):
        high = total.astype(BF16).astype(F32)
        low = total - high
        fine = dot(weight_three, jnp.concatenate([high, high, low], axis=0).astype(BF16))
        value = fine * slope2[q]
        sc[q + 1] = value.astype(BF16)
        kept = jnp.where(lane64 == q, turn(value[:, :LANES], q), strip[...])
        strip[...] = jnp.where(lane64 == q + 32, turn(value[:, LANES:], q + 33), kept)
        both = dot_nt(jnp.concatenate([high, low], axis=0).astype(BF16), feat[q])
        return head_sum + both[0:8] + both[8:16]

    def row_of(number, q):
        return srecv[number, pl.ds(pl.multiple_of(q * COUT, COUT), COUT), :]

    def cot_low(q, head_sum):
        total = row_of(0, q) + row_of(1, q) + pad[16 + q - start]
        return cot_step(q, total, head_sum)

    def cot_high(q, head_sum):
        total = row_of(2, q - 16) + pad[16 + q - start]
        return cot_step(q, total, head_sum)

    head_sum = lax.fori_loop(0, 16, cot_low, jnp.zeros((COUT, CF), F32), unroll=8)
    head_sum = lax.fori_loop(16, 32, cot_high, head_sum, unroll=8)
    strips_own = strips.at[len(ROW_NEIGHBOURS)]
    strips_own[...] = strip[...].astype(BF16)
    cot_copies = [
        send(sc.at[1], sc.at[33], (0, -1)),
        send(sc.at[32], sc.at[0], (0, 1)),
    ]
    for number, offset in enumerate(ROW_NEIGHBOURS):
        cot_copies.append(send(strips_own, strips.at[number], offset))

    for copy in value_copies:
        copy.wait_recv()

    def sample(step):
        here = pl.ds(pl.multiple_of(step * POINT_TILE, POINT_TILE), POINT_TILE)
        slot = slot_ref[0:1, here]
        along, across = frac_ref[0:1, here], frac_ref[1:2, here]
        rows, larger = row_weights(slot, along)
        columns = dot(table[...].reshape(64 * COUT, 256), rows).reshape(64, COUT, POINT_TILE)
        column = jnp.broadcast_to(slot >> 8, (COUT, POINT_TILE))[None]
        number = lax.broadcasted_iota(jnp.int32, (64, COUT, POINT_TILE), 0)
        away = number - column
        near = jnp.broadcast_to((1.0 - across) * larger, (COUT, POINT_TILE))[None]
        far = jnp.broadcast_to(across * larger, (COUT, POINT_TILE))[None]
        weights = jnp.where(away == 0, near, jnp.where(away == 1, far, 0.0))
        head_ref[:, here] = jnp.sum(weights * columns, axis=0)

    tiles = slot_ref.shape[1] // POINT_TILE
    cuts = [0] + [tiles * part // 8 for part in SAMPLE_CUTS] + [tiles]
    segments = iter(zip(cuts[:-1], cuts[1:]))

    def sample_next():
        first, last = next(segments)
        pl.loop(first, last)(sample)

    sample_next()

    for copy in cot_copies:
        copy.wait_recv()
    upper = jnp.where(between(1, 33, lane64), turn(arrived(strips, -1, 0), -31), 0.0)
    upper = jnp.where(lane64 == 0, turn(arrived(strips, -1, -1), -63), upper)
    upper = jnp.where(lane64 == 33, turn(arrived(strips, -1, 1), 1), upper) * above
    lower = jnp.where(between(65, 97, lane64), turn(arrived(strips, 1, 0), 65), 0.0)
    lower = jnp.where(lane64 == 64, turn(arrived(strips, 1, -1), 33), lower)
    lower = jnp.where(lane64 == 97, turn(arrived(strips, 1, 1), 97), lower) * below
    cot_rim = upper + lower

    def back_step(w):
        value = sc[w].astype(F32)
        even, odd = value[:, :LANES], value[:, LANES:]
        last = jnp.where(lane64 == 127, turn(cot_rim, 63 - w), turn(even, -1))
        first = jnp.where(lane64 == 0, turn(cot_rim, LANES - w), turn(odd, 1))
        taps = jnp.concatenate(
            [jnp.concatenate([odd, last], axis=1), value, jnp.concatenate([first, even], axis=1)],
            axis=0,
        ).astype(BF16)
        zbuf[w] = dot(backw[...], taps)
        return taps

    mixacc[...] = jnp.zeros_like(mixacc)
    back_step(0)

    @pl.loop(1, 33, unroll=8)
    def _(w):
        taps = back_step(w)
        mixacc[...] += dot_nt(taps, hid[pl.ds(w, 3)].reshape(192, 256))

    back_step(33)

    upacc[...] = jnp.zeros_like(upacc)

    @pl.loop(0, 8, unroll=8)
    def _(step):
        evens, odds = [], []
        for k in range(2):
            even_parts, odd_parts = [], []
            for parity in range(2):
                q = 4 * step + 2 * k + parity
                total = zbuf[q + 2, 0:64] + zbuf[q + 1, 64:128] + zbuf[q, 128:192]
                value = (total * slope1[q + 2]).astype(BF16)
                even_parts.append(value[:, :LANES])
                odd_parts.append(value[:, LANES:])
            evens.append(jnp.concatenate(even_parts, axis=0))
            odds.append(jnp.concatenate(odd_parts, axis=0))
        even = jnp.concatenate(evens, axis=1)
        odd = jnp.concatenate(odds, axis=1)

        def window(buffer):
            pair = [buffer[pl.ds(2 * step + 1 + k, 2)].reshape(2 * CIN, LANES) for k in range(2)]
            return jnp.concatenate(pair, axis=1)

        plain, moved = window(ext), window(exts)
        upacc[0] += dot_nt(odd, moved)
        upacc[1] += dot_nt(even, plain)
        upacc[2] += dot_nt(odd, plain)

    for row_tap in range(3):
        for col_tap, rows, lanes in ((0, 64, 128), (1, 0, 0), (2, 64, 0)):
            at = (col_tap * 3 + row_tap) * CF
            grads[at : at + CF] = upacc[row_tap, rows : rows + CF, lanes : lanes + LANES]
    grads[MIX_ROW : MIX_ROW + 192] = mixacc[:, :LANES]
    grads[MIX_ROW + 192 : HEAD_ROW] = jnp.concatenate(
        [mixacc[:, LANES:], jnp.zeros((192, CF), F32)], axis=1
    )
    grads[HEAD_ROW : HEAD_ROW + COUT] = jnp.concatenate(
        [head_sum, jnp.zeros((COUT, CF), F32)], axis=1
    )
    grads[HEAD_ROW + COUT :] = jnp.zeros((GRAD_ROWS - HEAD_ROW - COUT, LANES), F32)

    half = GRAD_ROWS // 2
    piece = half // chips

    def rows(start, size):
        return pl.ds(pl.multiple_of(start, 8), size)

    def part(number, source, target, peer):
        return pltpu.make_async_remote_copy(
            src_ref=source, dst_ref=target,
            send_sem=sum_send.at[number], recv_sem=sum_recv.at[number],
            device_id=peer, device_id_type=MESH,
        )

    base = core * half
    own = rows(here_chip * piece, piece)
    own_final = final.at[rows(base + here_chip * piece, piece)]

    def spread_part(k):
        number, peer = chip_at(k)
        return part(k, total.at[rows(number * piece, piece)], parts.at[k - 1], peer)

    def share_part(k):
        return part(chips + k, own_final, own_final, chip_at(k)[1])

    first = part(0, grads.at[rows((1 - core) * half, half)], other, core_peer)
    first.start()
    sample_next()
    first.wait_recv()
    total[...] = grads[rows(base, half)] + other[...]

    pl.loop(1, chips)(lambda k: spread_part(k).start())
    sample_next()
    pl.loop(1, chips)(lambda k: spread_part(k).wait_recv())
    final[rows(base + here_chip * piece, piece)] = total[own] + jnp.sum(parts[...], axis=0)

    pl.loop(1, chips)(lambda k: share_part(k).start())
    sample_next()
    pl.loop(1, chips)(lambda k: share_part(k).wait_recv())
    half_final = final.at[rows(base, half)]
    last = part(chips, half_final, half_final, core_peer)
    last.start()
    last.wait_recv()

    up_ref[...] = final[:MIX_ROW]
    for col_tap in range(3):
        for row_tap in range(3):
            at = MIX_ROW + (col_tap // 2) * 192 + row_tap * CF
            lanes = (col_tap % 2) * CF
            to = (col_tap * 3 + row_tap) * CF
            mix_ref[to : to + CF] = final[at : at + CF, lanes : lanes + CF]
    headg_ref[...] = final[HEAD_ROW : HEAD_ROW + COUT, :CF]
    first.wait_send()
    last.wait_send()

    @pl.loop(1, chips)
    def _(k):
        spread_part(k).wait_send()
        share_part(k).wait_send()

    for copy in copies:
        copy.wait_send()


def vmem(count):
    return [pl.BlockSpec(memory_space=pltpu.VMEM)] * count


def per_device(nf, npat, coarse, w_up, w_mix, w_head, send_index, slot_ids, fractions, head_cot):
    by_column = coarse.transpose(1, 0, 2)
    points = slot_ids.shape[1]
    run = COLS * COUT
    chips, half = nf * npat // 2, GRAD_ROWS // 2
    scratch = [
        pltpu.VMEM((COLS + 3, CIN, LANES), BF16),
        pltpu.VMEM((COLS + 2, CIN, LANES), BF16),
        pltpu.VMEM((len(NEIGHBOURS) + 1, CIN, LANES), BF16),
        pltpu.VMEM((6 * CF, 2 * CIN), BF16),
        pltpu.VMEM((3 * CF, 3 * CF), BF16),
        pltpu.VMEM((3 * CF, 3 * CF), BF16),
        pltpu.VMEM((36, CF, 256), BF16),
        pltpu.VMEM((36, CF, 256), F32),
        pltpu.VMEM((32, CF, 256), F32),
        pltpu.VMEM((32, CF, 256), BF16),
        pltpu.VMEM((32, COUT, 256), F32),
        pltpu.VMEM((16, 16, 256), BF16),
        pltpu.VMEM((32, 16, 256), BF16),
        pltpu.VMEM((4 * run, 256), F32),
        pltpu.VMEM((3, run, 256), F32),
        pltpu.VMEM((48, COUT, 256), F32),
        pltpu.VMEM((34, CF, 256), BF16),
        pltpu.VMEM((CF, LANES), F32),
        pltpu.VMEM((len(ROW_NEIGHBOURS) + 1, CF, LANES), BF16),
        pltpu.VMEM((34, 3 * CF, 256), F32),
        pltpu.VMEM((3 * CF, 3 * CF), F32),
        pltpu.VMEM((3, 2 * CF, 2 * CIN), F32),
        pltpu.SMEM((4, LANES), jnp.int32),
        pltpu.SemaphoreType.DMA,
        pltpu.VMEM((GRAD_ROWS, LANES), F32),
        pltpu.VMEM((GRAD_ROWS, LANES), F32),
        pltpu.VMEM((half, LANES), F32),
        pltpu.VMEM((half, LANES), F32),
        pltpu.VMEM((chips - 1, half // chips, LANES), F32),
        pltpu.SemaphoreType.DMA((2 * chips,)),
        pltpu.SemaphoreType.DMA((2 * chips,)),
        pltpu.SemaphoreType.DMA((24,)),
        pltpu.SemaphoreType.DMA((24,)),
    ]
    head, up, mix, head_grad = pl.pallas_call(
        functools.partial(local_kernel, nf, npat),
        out_shape=(
            jax.ShapeDtypeStruct((COUT, points), F32),
            jax.ShapeDtypeStruct((9 * CF, CIN), F32),
            jax.ShapeDtypeStruct((9 * CF, CF), F32),
            jax.ShapeDtypeStruct((COUT, CF), F32),
        ),
        in_specs=[pl.BlockSpec(memory_space=pl.ANY)] + vmem(7),
        out_specs=tuple(vmem(4)),
        scratch_shapes=scratch,
        compiler_params=pltpu.CompilerParams(
            collective_id=0, has_side_effects=True, vmem_limit_bytes=56 * 2**20
        ),
        name="local",
    )(send_index, by_column, w_up, w_mix, w_head, slot_ids, fractions, head_cot)

    return head, up.reshape(3, 3, CF, CIN), mix.reshape(3, 3, CF, CF), head_grad


def solution(mesh):
    placed = (
        P(None, "patch", "face"),
        P(),
        P(),
        P(),
        P("face", "patch", None),
        P(None, ("face", "patch")),
        P(None, ("face", "patch")),
        P(None, ("face", "patch")),
    )
    return jax.shard_map(
        functools.partial(per_device, mesh.shape["face"], mesh.shape["patch"]),
        mesh=mesh,
        in_specs=placed,
        out_specs=(P(None, ("face", "patch")), P(), P(), P()),
        check_vma=False,
    )
```

```python
import functools

import jax
import jax.numpy as jnp
from jax import lax
from jax.experimental import pallas as pl
from jax.experimental.pallas import tpu as pltpu
from jax.sharding import PartitionSpec as P

MESH = pl.DeviceIdType.MESH
F32 = jnp.float32
BF16 = jnp.bfloat16

LANES = 128
CIN = 128
CF = 64
COUT = 8
COLS = 16
POINT_TILE = 2048
SAMPLE_CUTS = (3, 5, 7)
GRAD_ROWS = 1024
MIX_ROW = 9 * CF
HEAD_ROW = MIX_ROW + 6 * CF
NEIGHBOURS = tuple((df, dp) for df in (-1, 0, 1) for dp in (-1, 0, 1) if (df, dp) != (0, 0))
ROW_NEIGHBOURS = tuple(pair for pair in NEIGHBOURS if pair[0] != 0)


def dot(left, right):
    return lax.dot_general(left, right, (((1,), (0,)), ((), ())), preferred_element_type=F32)


def dot_nt(left, right):
    return lax.dot_general(left, right, (((1,), (1,)), ((), ())), preferred_element_type=F32)


def turn(value, steps):
    if isinstance(steps, int):
        steps = steps % LANES
        if steps == 0:
            return value
    return pltpu.roll(value, steps, axis=1)


def sigmoid(value):
    return 0.5 * jnp.tanh(0.5 * value) + 0.5


def row_weights(slot, along):
    width = slot.shape[1]
    larger = jnp.maximum(along, 1.0 - along)
    upper, lower = along / larger, (1.0 - along) / larger
    place = lax.broadcasted_iota(jnp.int32, (256, width), 0)
    natural = 2 * (place & 127) + (place >> 7)
    away = natural - (slot & 255)
    weight = jnp.where(away == 0, lower, jnp.where(away == 1, upper, 0.0))
    return weight.astype(BF16), larger


def local_kernel(
    nf, npat,
    send_ref, coarse_ref, wup_ref, wmix_ref, whead_ref,
    slot_ref, frac_ref, cot_ref,
    head_ref, up_ref, mix_ref, headg_ref,
    ext, exts, edges, upw, mixw, backw, hid, slope1, slope2, feat, gown, gsend, table,
    sacc, srecv, pad, sc, strip, strips, zbuf, mixacc, upacc, starts, start_sem,
    grads, final, total, other, parts, sum_send, sum_recv,
    send_sem, recv_sem,
):
    me_f, me_p = lax.axis_index("face"), lax.axis_index("patch")

    def device(df, dp):
        return (lax.rem(me_f + df + nf, nf), lax.rem(me_p + dp + npat, npat))

    start_copy = pltpu.make_async_copy(send_ref.at[0, :, pl.ds(0, LANES)], starts, start_sem)
    start_copy.start()
    barrier = pltpu.get_barrier_semaphore()
    partners = NEIGHBOURS + ((0, 2), (0, -2))
    chips = nf * npat // 2
    core = lax.rem(me_p, 2)
    here_chip = me_f * (npat // 2) + me_p // 2
    core_peer = (me_f, me_p + 1 - 2 * core)

    def chip_at(k):
        face = lax.rem(me_f + k // (npat // 2), nf)
        pair = lax.rem(me_p // 2 + k % (npat // 2), npat // 2)
        return face * (npat // 2) + pair, (face, 2 * pair + core)

    for df, dp in partners:
        pl.semaphore_signal(barrier, inc=1, device_id=device(df, dp), device_id_type=MESH)
    pl.semaphore_signal(barrier, inc=1, device_id=core_peer, device_id_type=MESH)

    @pl.loop(1, chips)
    def _(k):
        pl.semaphore_signal(barrier, inc=1, device_id=chip_at(k)[1], device_id_type=MESH)

    pl.semaphore_wait(barrier, len(partners) + chips)

    copies = []

    def send(source, target, offset):
        number = len(copies)
        copy = pltpu.make_async_remote_copy(
            src_ref=source, dst_ref=target,
            send_sem=send_sem.at[number], recv_sem=recv_sem.at[number],
            device_id=device(*offset), device_id_type=MESH,
        )
        copy.start()
        copies.append(copy)
        return copy

    lane = lax.broadcasted_iota(jnp.int32, (CIN, LANES), 1)
    lane64 = lane[:CF]
    ext[1 : COLS + 1] = jnp.swapaxes(coarse_ref[...], 0, 1)
    edge = jnp.zeros((CIN, LANES), F32)
    for j in range(COLS):
        column = ext[j + 1].astype(F32)
        edge = jnp.where(lane == j, turn(column, j), edge)
        edge = jnp.where(lane == COLS + j, turn(column, COLS + 1 + j), edge)
    edge_own = edges.at[len(NEIGHBOURS)]
    edge_own[...] = edge.astype(BF16)
    coarse_copies = [
        send(ext.at[1], ext.at[COLS + 1], (0, -1)),
        send(ext.at[COLS], ext.at[0], (0, 1)),
    ]
    for number, offset in enumerate(NEIGHBOURS):
        coarse_copies.append(send(edge_own, edges.at[number], offset))

    ext[COLS + 2] = jnp.zeros((CIN, LANES), BF16)
    for row_tap in range(3):
        low = slice(row_tap * CF, (row_tap + 1) * CF)
        high = slice((3 + row_tap) * CF, (4 + row_tap) * CF)
        upw[low, :CIN] = wup_ref[1, row_tap]
        upw[low, CIN:] = jnp.zeros((CF, CIN), BF16)
        upw[high, :CIN] = wup_ref[2, row_tap]
        upw[high, CIN:] = wup_ref[0, row_tap]
    mix_rows = [
        jnp.concatenate([wmix_ref[col_tap, row_tap].astype(F32) for col_tap in range(3)], axis=1)
        for row_tap in range(3)
    ]
    mixing = jnp.concatenate(mix_rows, axis=0)
    mixw[...] = mixing.astype(BF16)
    backw[...] = mixing.T.astype(BF16)

    sacc[...] = jnp.zeros_like(sacc)

    @pl.loop(0, slot_ref.shape[1] // POINT_TILE)
    def _(step):
        here = pl.ds(pl.multiple_of(step * POINT_TILE, POINT_TILE), POINT_TILE)
        slot = slot_ref[0:1, here]
        along, across = frac_ref[0:1, here], frac_ref[1:2, here]
        rows, larger = row_weights(slot, along)
        cot = cot_ref[:, here] * larger
        near, far = cot * (1.0 - across), cot * across
        column = jnp.broadcast_to(slot >> 8, near.shape)[None]
        number = lax.broadcasted_iota(jnp.int32, (64,) + near.shape, 0)
        away = number - column
        terms = jnp.where(away == 0, near[None], jnp.where(away == 1, far[None], 0.0))
        sacc[...] += dot_nt(terms.reshape(64 * COUT, POINT_TILE).astype(BF16), rows)

    run = COLS * COUT
    pad[0:16] = jnp.zeros((16, COUT, 256), F32)
    pad[16:32] = sacc[2 * run : 3 * run].reshape(16, COUT, 256)
    pad[32:48] = jnp.zeros((16, COUT, 256), F32)
    back_copies = [
        send(sacc.at[0:run], srecv.at[0], (0, 2)),
        send(sacc.at[run : 2 * run], srecv.at[1], (0, 1)),
        send(sacc.at[3 * run : 4 * run], srecv.at[2], (0, -1)),
    ]

    for copy in coarse_copies:
        copy.wait_recv()
    above = jnp.where(me_f > 0, 1.0, 0.0).astype(F32)
    below = jnp.where(me_f < nf - 1, 1.0, 0.0).astype(F32)

    def arrived(buffer, df, dp):
        pairs = NEIGHBOURS if buffer is edges else ROW_NEIGHBOURS
        return buffer[pairs.index((-df, -dp))].astype(F32)

    def between(low, high, index):
        return jnp.logical_and(index >= low, index < high)

    top = jnp.where(between(1, 17, lane), turn(arrived(edges, -1, 0), -15), 0.0)
    top = jnp.where(lane == 0, turn(arrived(edges, -1, -1), -31), top)
    top = jnp.where(lane == 17, turn(arrived(edges, -1, 1), 1), top) * above
    first_row = jnp.where(between(33, 49, lane), turn(edge, 33), 0.0)
    first_row = jnp.where(lane == 32, turn(arrived(edges, 0, -1), 17), first_row)
    first_row = jnp.where(lane == 49, turn(arrived(edges, 0, 1), 49), first_row)
    bottom = jnp.where(between(65, 81, lane), turn(arrived(edges, 1, 0), 65), 0.0)
    bottom = jnp.where(lane == 64, turn(arrived(edges, 1, -1), 49), bottom)
    bottom = jnp.where(lane == 81, turn(arrived(edges, 1, 1), 81), bottom) * below
    rim = top + first_row + bottom
    rim_pair = jnp.concatenate([rim, turn(rim, -1)], axis=0).astype(BF16)
    rim_out = dot(upw[...], rim_pair)
    rim_hidden = []
    for parity in range(2):
        part = rim_out[parity * 192 : (parity + 1) * 192]
        upper = part[128:192] + turn(part[0:64], -32)
        value = jnp.where(lane64 < 32, upper * above, jnp.where(between(64, 96, lane64), part[64:128], 0.0))
        rim_hidden.append(value * sigmoid(value))
    even_rim, odd_rim = rim_hidden
    mix_rim = [
        dot(mixw[...], jnp.concatenate([turn(odd_rim, 1), even_rim, odd_rim], axis=0).astype(BF16)),
        dot(mixw[...], jnp.concatenate([even_rim, odd_rim, turn(even_rim, -1)], axis=0).astype(BF16)),
    ]

    @pl.loop(0, 9, unroll=9)
    def _(step):
        t = 2 * step
        pair = [ext[pl.ds(t + k, 2)].reshape(2 * CIN, LANES) for k in range(2)]
        out = dot(upw[...], jnp.concatenate(pair, axis=1))
        for k in range(2):
            here = t + k
            for parity in range(2):
                part = out[parity * 192 : (parity + 1) * 192, k * LANES : (k + 1) * LANES]
                entering = turn(rim_out[parity * 192 : parity * 192 + 64], 63 - here)
                odd = part[128:192] + jnp.where(lane64 == 127, entering, turn(part[0:64], -1))
                value = jnp.concatenate([part[64:128], odd], axis=1)
                sigma = sigmoid(value)
                hid[2 * here + parity] = (value * sigma).astype(BF16)
                slope1[2 * here + parity] = sigma * (1.0 + value * (1.0 - sigma))
            shifted = turn(ext[here].astype(F32), -1)
            exts[here] = jnp.where(lane == 127, turn(rim, 63 - here), shifted).astype(BF16)

    weight = whead_ref[...]
    weight_high = weight.astype(BF16).astype(F32)
    head_pair = jnp.concatenate([weight_high, weight - weight_high], axis=0).astype(BF16)

    def mix_step(j):
        values = []
        for parity in range(2):
            q = 2 * j + parity
            out = dot(mixw[...], hid[pl.ds(q + 1, 3)].reshape(192, 256))
            low, mid, high = out[0:64], out[64:128], out[128:192]
            first = turn(mix_rim[parity][0:64], 127 - j)
            last = turn(mix_rim[parity][128:192], 62 - j)
            even = jnp.where(lane64 == 0, first, turn(low[:, LANES:], 1)) + mid[:, :LANES] + high[:, LANES:]
            odd = low[:, :LANES] + mid[:, LANES:] + jnp.where(lane64 == 127, last, turn(high[:, :LANES], -1))
            value = jnp.concatenate([even, odd], axis=1)
            sigma = sigmoid(value)
            feature = (value * sigma).astype(BF16)
            feat[q] = feature
            slope2[q] = sigma * (1.0 + value * (1.0 - sigma))
            both = dot(head_pair, feature)
            point_value = both[0:8] + both[8:16]
            gown[q] = point_value
            values.append(point_value)
        gsend[j] = jnp.concatenate(values, axis=0).astype(BF16)

    pl.loop(0, 8, unroll=8)(mix_step)
    value_copies = [
        send(gsend.at[0:8], table.at[0:8], (0, -2)),
        send(gsend.at[0:8], table.at[8:16], (0, -1)),
    ]
    pl.loop(8, 16, unroll=8)(mix_step)
    value_copies.append(send(gsend.at[8:16], table.at[24:32], (0, 1)))

    start_copy.wait()
    start = starts[2, 0] // 256
    for k in range(8):
        pair = [gown[start + 2 * k], gown[start + 2 * k + 1]]
        table[16 + k] = jnp.concatenate(pair, axis=0).astype(BF16)

    for copy in back_copies:
        copy.wait_recv()
    weight_t = whead_ref[...].T
    high_t = weight_t.astype(BF16).astype(F32)
    weight_three = jnp.concatenate([high_t, weight_t - high_t, high_t], axis=1).astype(BF16)
    strip[...] = jnp.zeros_like(strip)

    def cot_step(q, total, head_sum):
        high = total.astype(BF16).astype(F32)
        low = total - high
        fine = dot(weight_three, jnp.concatenate([high, high, low], axis=0).astype(BF16))
        value = fine * slope2[q]
        sc[q + 1] = value.astype(BF16)
        kept = jnp.where(lane64 == q, turn(value[:, :LANES], q), strip[...])
        strip[...] = jnp.where(lane64 == q + 32, turn(value[:, LANES:], q + 33), kept)
        both = dot_nt(jnp.concatenate([high, low], axis=0).astype(BF16), feat[q])
        return head_sum + both[0:8] + both[8:16]

    def row_of(number, q):
        return srecv[number, pl.ds(pl.multiple_of(q * COUT, COUT), COUT), :]

    def cot_low(q, head_sum):
        total = row_of(0, q) + row_of(1, q) + pad[16 + q - start]
        return cot_step(q, total, head_sum)

    def cot_high(q, head_sum):
        total = row_of(2, q - 16) + pad[16 + q - start]
        return cot_step(q, total, head_sum)

    head_sum = lax.fori_loop(0, 16, cot_low, jnp.zeros((COUT, CF), F32), unroll=8)
    head_sum = lax.fori_loop(16, 32, cot_high, head_sum, unroll=8)
    strips_own = strips.at[len(ROW_NEIGHBOURS)]
    strips_own[...] = strip[...].astype(BF16)
    cot_copies = [
        send(sc.at[1], sc.at[33], (0, -1)),
        send(sc.at[32], sc.at[0], (0, 1)),
    ]
    for number, offset in enumerate(ROW_NEIGHBOURS):
        cot_copies.append(send(strips_own, strips.at[number], offset))

    for copy in value_copies:
        copy.wait_recv()

    def sample(step):
        here = pl.ds(pl.multiple_of(step * POINT_TILE, POINT_TILE), POINT_TILE)
        slot = slot_ref[0:1, here]
        along, across = frac_ref[0:1, here], frac_ref[1:2, here]
        rows, larger = row_weights(slot, along)
        columns = dot(table[...].reshape(64 * COUT, 256), rows).reshape(64, COUT, POINT_TILE)
        column = jnp.broadcast_to(slot >> 8, (COUT, POINT_TILE))[None]
        number = lax.broadcasted_iota(jnp.int32, (64, COUT, POINT_TILE), 0)
        away = number - column
        near = jnp.broadcast_to((1.0 - across) * larger, (COUT, POINT_TILE))[None]
        far = jnp.broadcast_to(across * larger, (COUT, POINT_TILE))[None]
        weights = jnp.where(away == 0, near, jnp.where(away == 1, far, 0.0))
        head_ref[:, here] = jnp.sum(weights * columns, axis=0)

    tiles = slot_ref.shape[1] // POINT_TILE
    cuts = [0] + [tiles * part // 8 for part in SAMPLE_CUTS] + [tiles]
    segments = iter(zip(cuts[:-1], cuts[1:]))

    def sample_next():
        first, last = next(segments)
        pl.loop(first, last)(sample)

    sample_next()

    for copy in cot_copies:
        copy.wait_recv()
    upper = jnp.where(between(1, 33, lane64), turn(arrived(strips, -1, 0), -31), 0.0)
    upper = jnp.where(lane64 == 0, turn(arrived(strips, -1, -1), -63), upper)
    upper = jnp.where(lane64 == 33, turn(arrived(strips, -1, 1), 1), upper) * above
    lower = jnp.where(between(65, 97, lane64), turn(arrived(strips, 1, 0), 65), 0.0)
    lower = jnp.where(lane64 == 64, turn(arrived(strips, 1, -1), 33), lower)
    lower = jnp.where(lane64 == 97, turn(arrived(strips, 1, 1), 97), lower) * below
    cot_rim = upper + lower

    def back_step(w):
        value = sc[w].astype(F32)
        even, odd = value[:, :LANES], value[:, LANES:]
        last = jnp.where(lane64 == 127, turn(cot_rim, 63 - w), turn(even, -1))
        first = jnp.where(lane64 == 0, turn(cot_rim, LANES - w), turn(odd, 1))
        taps = jnp.concatenate(
            [jnp.concatenate([odd, last], axis=1), value, jnp.concatenate([first, even], axis=1)],
            axis=0,
        ).astype(BF16)
        zbuf[w] = dot(backw[...], taps)
        return taps

    mixacc[...] = jnp.zeros_like(mixacc)
    back_step(0)

    @pl.loop(1, 33, unroll=8)
    def _(w):
        taps = back_step(w)
        mixacc[...] += dot_nt(taps, hid[pl.ds(w, 3)].reshape(192, 256))

    back_step(33)

    upacc[...] = jnp.zeros_like(upacc)

    @pl.loop(0, 8, unroll=8)
    def _(step):
        evens, odds = [], []
        for k in range(2):
            even_parts, odd_parts = [], []
            for parity in range(2):
                q = 4 * step + 2 * k + parity
                total = zbuf[q + 2, 0:64] + zbuf[q + 1, 64:128] + zbuf[q, 128:192]
                value = (total * slope1[q + 2]).astype(BF16)
                even_parts.append(value[:, :LANES])
                odd_parts.append(value[:, LANES:])
            evens.append(jnp.concatenate(even_parts, axis=0))
            odds.append(jnp.concatenate(odd_parts, axis=0))
        even = jnp.concatenate(evens, axis=1)
        odd = jnp.concatenate(odds, axis=1)

        def window(buffer):
            pair = [buffer[pl.ds(2 * step + 1 + k, 2)].reshape(2 * CIN, LANES) for k in range(2)]
            return jnp.concatenate(pair, axis=1)

        plain, moved = window(ext), window(exts)
        upacc[0] += dot_nt(odd, moved)
        upacc[1] += dot_nt(even, plain)
        upacc[2] += dot_nt(odd, plain)

    for row_tap in range(3):
        for col_tap, rows, lanes in ((0, 64, 128), (1, 0, 0), (2, 64, 0)):
            at = (col_tap * 3 + row_tap) * CF
            grads[at : at + CF] = upacc[row_tap, rows : rows + CF, lanes : lanes + LANES]
    grads[MIX_ROW : MIX_ROW + 192] = mixacc[:, :LANES]
    grads[MIX_ROW + 192 : HEAD_ROW] = jnp.concatenate(
        [mixacc[:, LANES:], jnp.zeros((192, CF), F32)], axis=1
    )
    grads[HEAD_ROW : HEAD_ROW + COUT] = jnp.concatenate(
        [head_sum, jnp.zeros((COUT, CF), F32)], axis=1
    )
    grads[HEAD_ROW + COUT :] = jnp.zeros((GRAD_ROWS - HEAD_ROW - COUT, LANES), F32)

    half = GRAD_ROWS // 2
    piece = half // chips

    def rows(start, size):
        return pl.ds(pl.multiple_of(start, 8), size)

    def part(number, source, target, peer):
        return pltpu.make_async_remote_copy(
            src_ref=source, dst_ref=target,
            send_sem=sum_send.at[number], recv_sem=sum_recv.at[number],
            device_id=peer, device_id_type=MESH,
        )

    base = core * half
    own = rows(here_chip * piece, piece)
    own_final = final.at[rows(base + here_chip * piece, piece)]

    def spread_part(k):
        number, peer = chip_at(k)
        return part(k, total.at[rows(number * piece, piece)], parts.at[k - 1], peer)

    def share_part(k):
        return part(chips + k, own_final, own_final, chip_at(k)[1])

    first = part(0, grads.at[rows((1 - core) * half, half)], other, core_peer)
    first.start()
    sample_next()
    first.wait_recv()
    total[...] = grads[rows(base, half)] + other[...]

    pl.loop(1, chips)(lambda k: spread_part(k).start())
    sample_next()
    pl.loop(1, chips)(lambda k: spread_part(k).wait_recv())
    final[rows(base + here_chip * piece, piece)] = total[own] + jnp.sum(parts[...], axis=0)

    pl.loop(1, chips)(lambda k: share_part(k).start())
    sample_next()
    pl.loop(1, chips)(lambda k: share_part(k).wait_recv())
    half_final = final.at[rows(base, half)]
    last = part(chips, half_final, half_final, core_peer)
    last.start()
    last.wait_recv()

    up_ref[...] = final[:MIX_ROW]
    for col_tap in range(3):
        for row_tap in range(3):
            at = MIX_ROW + (col_tap // 2) * 192 + row_tap * CF
            lanes = (col_tap % 2) * CF
            to = (col_tap * 3 + row_tap) * CF
            mix_ref[to : to + CF] = final[at : at + CF, lanes : lanes + CF]
    headg_ref[...] = final[HEAD_ROW : HEAD_ROW + COUT, :CF]
    first.wait_send()
    last.wait_send()

    @pl.loop(1, chips)
    def _(k):
        spread_part(k).wait_send()
        share_part(k).wait_send()

    for copy in copies:
        copy.wait_send()


def move_kernel(*refs):
    count = len(refs) // 2
    for k in range(count):
        refs[count + k][...] = refs[k][...]


def vmem(count):
    return [pl.BlockSpec(memory_space=pltpu.VMEM)] * count


def per_device(nf, npat, coarse, w_up, w_mix, w_head, send_index, slot_ids, fractions, head_cot):
    points = slot_ids.shape[1]
    run = COLS * COUT
    chips, half = nf * npat // 2, GRAD_ROWS // 2
    scratch = [
        pltpu.VMEM((COLS + 3, CIN, LANES), BF16),
        pltpu.VMEM((COLS + 2, CIN, LANES), BF16),
        pltpu.VMEM((len(NEIGHBOURS) + 1, CIN, LANES), BF16),
        pltpu.VMEM((6 * CF, 2 * CIN), BF16),
        pltpu.VMEM((3 * CF, 3 * CF), BF16),
        pltpu.VMEM((3 * CF, 3 * CF), BF16),
        pltpu.VMEM((36, CF, 256), BF16),
        pltpu.VMEM((36, CF, 256), F32),
        pltpu.VMEM((32, CF, 256), F32),
        pltpu.VMEM((32, CF, 256), BF16),
        pltpu.VMEM((32, COUT, 256), F32),
        pltpu.VMEM((16, 16, 256), BF16),
        pltpu.VMEM((32, 16, 256), BF16),
        pltpu.VMEM((4 * run, 256), F32),
        pltpu.VMEM((3, run, 256), F32),
        pltpu.VMEM((48, COUT, 256), F32),
        pltpu.VMEM((34, CF, 256), BF16),
        pltpu.VMEM((CF, LANES), F32),
        pltpu.VMEM((len(ROW_NEIGHBOURS) + 1, CF, LANES), BF16),
        pltpu.VMEM((34, 3 * CF, 256), F32),
        pltpu.VMEM((3 * CF, 3 * CF), F32),
        pltpu.VMEM((3, 2 * CF, 2 * CIN), F32),
        pltpu.SMEM((4, LANES), jnp.int32),
        pltpu.SemaphoreType.DMA,
        pltpu.VMEM((GRAD_ROWS, LANES), F32),
        pltpu.VMEM((GRAD_ROWS, LANES), F32),
        pltpu.VMEM((half, LANES), F32),
        pltpu.VMEM((half, LANES), F32),
        pltpu.VMEM((chips - 1, half // chips, LANES), F32),
        pltpu.SemaphoreType.DMA((2 * chips,)),
        pltpu.SemaphoreType.DMA((2 * chips,)),
        pltpu.SemaphoreType.DMA((24,)),
        pltpu.SemaphoreType.DMA((24,)),
    ]
    head, up, mix, head_grad = pl.pallas_call(
        functools.partial(local_kernel, nf, npat),
        out_shape=(
            jax.ShapeDtypeStruct((COUT, points), F32),
            jax.ShapeDtypeStruct((9 * CF, CIN), F32),
            jax.ShapeDtypeStruct((9 * CF, CF), F32),
            jax.ShapeDtypeStruct((COUT, CF), F32),
        ),
        in_specs=[pl.BlockSpec(memory_space=pl.ANY)] + vmem(7),
        out_specs=tuple(vmem(4)),
        scratch_shapes=scratch,
        compiler_params=pltpu.CompilerParams(
            collective_id=0, has_side_effects=True, vmem_limit_bytes=56 * 2**20
        ),
        name="local",
    )(send_index, coarse, w_up, w_mix, w_head, slot_ids, fractions, head_cot)

    results = (head, up, mix, head_grad)
    head, up, mix, head_grad = pl.pallas_call(
        move_kernel,
        out_shape=tuple(jax.ShapeDtypeStruct(one.shape, one.dtype) for one in results),
        in_specs=vmem(4),
        out_specs=tuple(vmem(4)),
        compiler_params=pltpu.CompilerParams(vmem_limit_bytes=56 * 2**20),
        name="move",
    )(*results)
    return head, up.reshape(3, 3, CF, CIN), mix.reshape(3, 3, CF, CF), head_grad


def solution(mesh):
    placed = (
        P(None, "patch", "face"),
        P(),
        P(),
        P(),
        P("face", "patch", None),
        P(None, ("face", "patch")),
        P(None, ("face", "patch")),
        P(None, ("face", "patch")),
    )
    return jax.shard_map(
        functools.partial(per_device, mesh.shape["face"], mesh.shape["patch"]),
        mesh=mesh,
        in_specs=placed,
        out_specs=(P(None, ("face", "patch")), P(), P(), P()),
        check_vma=False,
    )
```

```python
import functools

import jax
import jax.numpy as jnp
from jax import lax
from jax.experimental import pallas as pl
from jax.experimental.pallas import tpu as pltpu
from jax.sharding import PartitionSpec as P

MESH = pl.DeviceIdType.MESH
F32 = jnp.float32
BF16 = jnp.bfloat16

LANES = 128
CIN = 128
CF = 64
COUT = 8
COLS = 16
POINT_TILE = 2048
EARLY = 2
SAMPLE_CUTS = (3, 5, 7)
GRAD_ROWS = 1024
MIX_ROW = 9 * CF
HEAD_ROW = MIX_ROW + 6 * CF
NEIGHBOURS = tuple((df, dp) for df in (-1, 0, 1) for dp in (-1, 0, 1) if (df, dp) != (0, 0))
ROW_NEIGHBOURS = tuple(pair for pair in NEIGHBOURS if pair[0] != 0)


def dot(left, right):
    return lax.dot_general(left, right, (((1,), (0,)), ((), ())), preferred_element_type=F32)


def dot_nt(left, right):
    return lax.dot_general(left, right, (((1,), (1,)), ((), ())), preferred_element_type=F32)


def turn(value, steps):
    if isinstance(steps, int):
        steps = steps % LANES
        if steps == 0:
            return value
    return pltpu.roll(value, steps, axis=1)


def sigmoid(value):
    return 0.5 * jnp.tanh(0.5 * value) + 0.5


def row_weights(slot, along):
    width = slot.shape[1]
    larger = jnp.maximum(along, 1.0 - along)
    upper, lower = along / larger, (1.0 - along) / larger
    place = lax.broadcasted_iota(jnp.int32, (256, width), 0)
    natural = 2 * (place & 127) + (place >> 7)
    away = natural - (slot & 255)
    weight = jnp.where(away == 0, lower, jnp.where(away == 1, upper, 0.0))
    return weight.astype(BF16), larger


def local_kernel(
    nf, npat,
    send_ref, coarse_ref, wup_ref, wmix_ref, whead_ref,
    slot_ref, frac_ref, cot_ref,
    head_ref, up_ref, mix_ref, headg_ref,
    ext, exts, edges, upw, mixw, backw, hid, slope1, slope2, feat, gown, gsend, table,
    sacc, srecv, pad, sc, strip, strips, zbuf, mixacc, upacc, starts, start_sem,
    grads, final, total, other, parts, sum_send, sum_recv,
    send_sem, recv_sem,
):
    me_f, me_p = lax.axis_index("face"), lax.axis_index("patch")

    def device(df, dp):
        return (lax.rem(me_f + df + nf, nf), lax.rem(me_p + dp + npat, npat))

    start_copy = pltpu.make_async_copy(send_ref.at[0, :, pl.ds(0, LANES)], starts, start_sem)
    start_copy.start()
    barrier = pltpu.get_barrier_semaphore()
    partners = NEIGHBOURS + ((0, 2), (0, -2))
    chips = nf * npat // 2
    core = lax.rem(me_p, 2)
    here_chip = me_f * (npat // 2) + me_p // 2
    core_peer = (me_f, me_p + 1 - 2 * core)

    def chip_at(k):
        face = lax.rem(me_f + k // (npat // 2), nf)
        pair = lax.rem(me_p // 2 + k % (npat // 2), npat // 2)
        return face * (npat // 2) + pair, (face, 2 * pair + core)

    for df, dp in partners:
        pl.semaphore_signal(barrier, inc=1, device_id=device(df, dp), device_id_type=MESH)
    pl.semaphore_signal(barrier, inc=1, device_id=core_peer, device_id_type=MESH)

    @pl.loop(1, chips)
    def _(k):
        pl.semaphore_signal(barrier, inc=1, device_id=chip_at(k)[1], device_id_type=MESH)


    copies = []

    def send(source, target, offset):
        number = len(copies)
        copy = pltpu.make_async_remote_copy(
            src_ref=source, dst_ref=target,
            send_sem=send_sem.at[number], recv_sem=recv_sem.at[number],
            device_id=device(*offset), device_id_type=MESH,
        )
        copy.start()
        copies.append(copy)
        return copy

    lane = lax.broadcasted_iota(jnp.int32, (CIN, LANES), 1)
    lane64 = lane[:CF]
    ext[1 : COLS + 1] = jnp.swapaxes(coarse_ref[...], 0, 1)
    edge = jnp.zeros((CIN, LANES), F32)
    for j in range(COLS):
        column = ext[j + 1].astype(F32)
        edge = jnp.where(lane == j, turn(column, j), edge)
        edge = jnp.where(lane == COLS + j, turn(column, COLS + 1 + j), edge)
    edge_own = edges.at[len(NEIGHBOURS)]
    edge_own[...] = edge.astype(BF16)
    ext[COLS + 2] = jnp.zeros((CIN, LANES), BF16)
    for row_tap in range(3):
        low = slice(row_tap * CF, (row_tap + 1) * CF)
        high = slice((3 + row_tap) * CF, (4 + row_tap) * CF)
        upw[low, :CIN] = wup_ref[1, row_tap]
        upw[low, CIN:] = jnp.zeros((CF, CIN), BF16)
        upw[high, :CIN] = wup_ref[2, row_tap]
        upw[high, CIN:] = wup_ref[0, row_tap]
    mix_rows = [
        jnp.concatenate([wmix_ref[col_tap, row_tap].astype(F32) for col_tap in range(3)], axis=1)
        for row_tap in range(3)
    ]
    mixing = jnp.concatenate(mix_rows, axis=0)
    mixw[...] = mixing.astype(BF16)
    backw[...] = mixing.T.astype(BF16)

    sacc[...] = jnp.zeros_like(sacc)

    def scatter(step):
        here = pl.ds(pl.multiple_of(step * POINT_TILE, POINT_TILE), POINT_TILE)
        slot = slot_ref[0:1, here]
        along, across = frac_ref[0:1, here], frac_ref[1:2, here]
        rows, larger = row_weights(slot, along)
        cot = cot_ref[:, here] * larger
        near, far = cot * (1.0 - across), cot * across
        column = jnp.broadcast_to(slot >> 8, near.shape)[None]
        number = lax.broadcasted_iota(jnp.int32, (64,) + near.shape, 0)
        away = number - column
        terms = jnp.where(away == 0, near[None], jnp.where(away == 1, far[None], 0.0))
        sacc[...] += dot_nt(terms.reshape(64 * COUT, POINT_TILE).astype(BF16), rows)

    tiles = slot_ref.shape[1] // POINT_TILE
    early = tiles * EARLY // 8
    pl.loop(0, early)(scatter)
    pl.semaphore_wait(barrier, len(partners) + chips)
    coarse_copies = [
        send(ext.at[1], ext.at[COLS + 1], (0, -1)),
        send(ext.at[COLS], ext.at[0], (0, 1)),
    ]
    for number, offset in enumerate(NEIGHBOURS):
        coarse_copies.append(send(edge_own, edges.at[number], offset))

    pl.loop(early, tiles)(scatter)

    run = COLS * COUT
    pad[0:16] = jnp.zeros((16, COUT, 256), F32)
    pad[16:32] = sacc[2 * run : 3 * run].reshape(16, COUT, 256)
    pad[32:48] = jnp.zeros((16, COUT, 256), F32)
    back_copies = [
        send(sacc.at[0:run], srecv.at[0], (0, 2)),
        send(sacc.at[run : 2 * run], srecv.at[1], (0, 1)),
        send(sacc.at[3 * run : 4 * run], srecv.at[2], (0, -1)),
    ]

    for copy in coarse_copies:
        copy.wait_recv()
    above = jnp.where(me_f > 0, 1.0, 0.0).astype(F32)
    below = jnp.where(me_f < nf - 1, 1.0, 0.0).astype(F32)

    def arrived(buffer, df, dp):
        pairs = NEIGHBOURS if buffer is edges else ROW_NEIGHBOURS
        return buffer[pairs.index((-df, -dp))].astype(F32)

    def between(low, high, index):
        return jnp.logical_and(index >= low, index < high)

    top = jnp.where(between(1, 17, lane), turn(arrived(edges, -1, 0), -15), 0.0)
    top = jnp.where(lane == 0, turn(arrived(edges, -1, -1), -31), top)
    top = jnp.where(lane == 17, turn(arrived(edges, -1, 1), 1), top) * above
    first_row = jnp.where(between(33, 49, lane), turn(edge, 33), 0.0)
    first_row = jnp.where(lane == 32, turn(arrived(edges, 0, -1), 17), first_row)
    first_row = jnp.where(lane == 49, turn(arrived(edges, 0, 1), 49), first_row)
    bottom = jnp.where(between(65, 81, lane), turn(arrived(edges, 1, 0), 65), 0.0)
    bottom = jnp.where(lane == 64, turn(arrived(edges, 1, -1), 49), bottom)
    bottom = jnp.where(lane == 81, turn(arrived(edges, 1, 1), 81), bottom) * below
    rim = top + first_row + bottom
    rim_pair = jnp.concatenate([rim, turn(rim, -1)], axis=0).astype(BF16)
    rim_out = dot(upw[...], rim_pair)
    rim_hidden = []
    for parity in range(2):
        part = rim_out[parity * 192 : (parity + 1) * 192]
        upper = part[128:192] + turn(part[0:64], -32)
        value = jnp.where(lane64 < 32, upper * above, jnp.where(between(64, 96, lane64), part[64:128], 0.0))
        rim_hidden.append(value * sigmoid(value))
    even_rim, odd_rim = rim_hidden
    mix_rim = [
        dot(mixw[...], jnp.concatenate([turn(odd_rim, 1), even_rim, odd_rim], axis=0).astype(BF16)),
        dot(mixw[...], jnp.concatenate([even_rim, odd_rim, turn(even_rim, -1)], axis=0).astype(BF16)),
    ]

    @pl.loop(0, 9, unroll=9)
    def _(step):
        t = 2 * step
        pair = [ext[pl.ds(t + k, 2)].reshape(2 * CIN, LANES) for k in range(2)]
        out = dot(upw[...], jnp.concatenate(pair, axis=1))
        for k in range(2):
            here = t + k
            for parity in range(2):
                part = out[parity * 192 : (parity + 1) * 192, k * LANES : (k + 1) * LANES]
                entering = turn(rim_out[parity * 192 : parity * 192 + 64], 63 - here)
                odd = part[128:192] + jnp.where(lane64 == 127, entering, turn(part[0:64], -1))
                value = jnp.concatenate([part[64:128], odd], axis=1)
                sigma = sigmoid(value)
                hid[2 * here + parity] = (value * sigma).astype(BF16)
                slope1[2 * here + parity] = sigma * (1.0 + value * (1.0 - sigma))
            shifted = turn(ext[here].astype(F32), -1)
            exts[here] = jnp.where(lane == 127, turn(rim, 63 - here), shifted).astype(BF16)

    weight = whead_ref[...]
    weight_high = weight.astype(BF16).astype(F32)
    head_pair = jnp.concatenate([weight_high, weight - weight_high], axis=0).astype(BF16)

    def mix_step(j):
        values = []
        for parity in range(2):
            q = 2 * j + parity
            out = dot(mixw[...], hid[pl.ds(q + 1, 3)].reshape(192, 256))
            low, mid, high = out[0:64], out[64:128], out[128:192]
            first = turn(mix_rim[parity][0:64], 127 - j)
            last = turn(mix_rim[parity][128:192], 62 - j)
            even = jnp.where(lane64 == 0, first, turn(low[:, LANES:], 1)) + mid[:, :LANES] + high[:, LANES:]
            odd = low[:, :LANES] + mid[:, LANES:] + jnp.where(lane64 == 127, last, turn(high[:, :LANES], -1))
            value = jnp.concatenate([even, odd], axis=1)
            sigma = sigmoid(value)
            feature = (value * sigma).astype(BF16)
            feat[q] = feature
            slope2[q] = sigma * (1.0 + value * (1.0 - sigma))
            both = dot(head_pair, feature)
            point_value = both[0:8] + both[8:16]
            gown[q] = point_value
            values.append(point_value)
        gsend[j] = jnp.concatenate(values, axis=0).astype(BF16)

    pl.loop(0, 8, unroll=8)(mix_step)
    value_copies = [
        send(gsend.at[0:8], table.at[0:8], (0, -2)),
        send(gsend.at[0:8], table.at[8:16], (0, -1)),
    ]
    pl.loop(8, 16, unroll=8)(mix_step)
    value_copies.append(send(gsend.at[8:16], table.at[24:32], (0, 1)))

    start_copy.wait()
    start = starts[2, 0] // 256
    for k in range(8):
        pair = [gown[start + 2 * k], gown[start + 2 * k + 1]]
        table[16 + k] = jnp.concatenate(pair, axis=0).astype(BF16)

    for copy in back_copies:
        copy.wait_recv()
    weight_t = whead_ref[...].T
    high_t = weight_t.astype(BF16).astype(F32)
    weight_three = jnp.concatenate([high_t, weight_t - high_t, high_t], axis=1).astype(BF16)
    strip[...] = jnp.zeros_like(strip)

    def cot_step(q, total, head_sum):
        high = total.astype(BF16).astype(F32)
        low = total - high
        fine = dot(weight_three, jnp.concatenate([high, high, low], axis=0).astype(BF16))
        value = fine * slope2[q]
        sc[q + 1] = value.astype(BF16)
        kept = jnp.where(lane64 == q, turn(value[:, :LANES], q), strip[...])
        strip[...] = jnp.where(lane64 == q + 32, turn(value[:, LANES:], q + 33), kept)
        both = dot_nt(jnp.concatenate([high, low], axis=0).astype(BF16), feat[q])
        return head_sum + both[0:8] + both[8:16]

    def row_of(number, q):
        return srecv[number, pl.ds(pl.multiple_of(q * COUT, COUT), COUT), :]

    def cot_low(q, head_sum):
        total = row_of(0, q) + row_of(1, q) + pad[16 + q - start]
        return cot_step(q, total, head_sum)

    def cot_high(q, head_sum):
        total = row_of(2, q - 16) + pad[16 + q - start]
        return cot_step(q, total, head_sum)

    head_sum = lax.fori_loop(0, 16, cot_low, jnp.zeros((COUT, CF), F32), unroll=8)
    head_sum = lax.fori_loop(16, 32, cot_high, head_sum, unroll=8)
    strips_own = strips.at[len(ROW_NEIGHBOURS)]
    strips_own[...] = strip[...].astype(BF16)
    cot_copies = [
        send(sc.at[1], sc.at[33], (0, -1)),
        send(sc.at[32], sc.at[0], (0, 1)),
    ]
    for number, offset in enumerate(ROW_NEIGHBOURS):
        cot_copies.append(send(strips_own, strips.at[number], offset))

    for copy in value_copies:
        copy.wait_recv()

    def sample(step):
        here = pl.ds(pl.multiple_of(step * POINT_TILE, POINT_TILE), POINT_TILE)
        slot = slot_ref[0:1, here]
        along, across = frac_ref[0:1, here], frac_ref[1:2, here]
        rows, larger = row_weights(slot, along)
        columns = dot(table[...].reshape(64 * COUT, 256), rows).reshape(64, COUT, POINT_TILE)
        column = jnp.broadcast_to(slot >> 8, (COUT, POINT_TILE))[None]
        number = lax.broadcasted_iota(jnp.int32, (64, COUT, POINT_TILE), 0)
        away = number - column
        near = jnp.broadcast_to((1.0 - across) * larger, (COUT, POINT_TILE))[None]
        far = jnp.broadcast_to(across * larger, (COUT, POINT_TILE))[None]
        weights = jnp.where(away == 0, near, jnp.where(away == 1, far, 0.0))
        head_ref[:, here] = jnp.sum(weights * columns, axis=0)

    tiles = slot_ref.shape[1] // POINT_TILE
    cuts = [0] + [tiles * part // 8 for part in SAMPLE_CUTS] + [tiles]
    segments = iter(zip(cuts[:-1], cuts[1:]))

    def sample_next():
        first, last = next(segments)
        pl.loop(first, last)(sample)

    sample_next()

    for copy in cot_copies:
        copy.wait_recv()
    upper = jnp.where(between(1, 33, lane64), turn(arrived(strips, -1, 0), -31), 0.0)
    upper = jnp.where(lane64 == 0, turn(arrived(strips, -1, -1), -63), upper)
    upper = jnp.where(lane64 == 33, turn(arrived(strips, -1, 1), 1), upper) * above
    lower = jnp.where(between(65, 97, lane64), turn(arrived(strips, 1, 0), 65), 0.0)
    lower = jnp.where(lane64 == 64, turn(arrived(strips, 1, -1), 33), lower)
    lower = jnp.where(lane64 == 97, turn(arrived(strips, 1, 1), 97), lower) * below
    cot_rim = upper + lower

    def back_step(w):
        value = sc[w].astype(F32)
        even, odd = value[:, :LANES], value[:, LANES:]
        last = jnp.where(lane64 == 127, turn(cot_rim, 63 - w), turn(even, -1))
        first = jnp.where(lane64 == 0, turn(cot_rim, LANES - w), turn(odd, 1))
        taps = jnp.concatenate(
            [jnp.concatenate([odd, last], axis=1), value, jnp.concatenate([first, even], axis=1)],
            axis=0,
        ).astype(BF16)
        zbuf[w] = dot(backw[...], taps)
        return taps

    mixacc[...] = jnp.zeros_like(mixacc)
    back_step(0)

    @pl.loop(1, 33, unroll=8)
    def _(w):
        taps = back_step(w)
        mixacc[...] += dot_nt(taps, hid[pl.ds(w, 3)].reshape(192, 256))

    back_step(33)

    upacc[...] = jnp.zeros_like(upacc)

    @pl.loop(0, 8, unroll=8)
    def _(step):
        evens, odds = [], []
        for k in range(2):
            even_parts, odd_parts = [], []
            for parity in range(2):
                q = 4 * step + 2 * k + parity
                total = zbuf[q + 2, 0:64] + zbuf[q + 1, 64:128] + zbuf[q, 128:192]
                value = (total * slope1[q + 2]).astype(BF16)
                even_parts.append(value[:, :LANES])
                odd_parts.append(value[:, LANES:])
            evens.append(jnp.concatenate(even_parts, axis=0))
            odds.append(jnp.concatenate(odd_parts, axis=0))
        even = jnp.concatenate(evens, axis=1)
        odd = jnp.concatenate(odds, axis=1)

        def window(buffer):
            pair = [buffer[pl.ds(2 * step + 1 + k, 2)].reshape(2 * CIN, LANES) for k in range(2)]
            return jnp.concatenate(pair, axis=1)

        plain, moved = window(ext), window(exts)
        upacc[0] += dot_nt(odd, moved)
        upacc[1] += dot_nt(even, plain)
        upacc[2] += dot_nt(odd, plain)

    for row_tap in range(3):
        for col_tap, rows, lanes in ((0, 64, 128), (1, 0, 0), (2, 64, 0)):
            at = (col_tap * 3 + row_tap) * CF
            grads[at : at + CF] = upacc[row_tap, rows : rows + CF, lanes : lanes + LANES]
    grads[MIX_ROW : MIX_ROW + 192] = mixacc[:, :LANES]
    grads[MIX_ROW + 192 : HEAD_ROW] = jnp.concatenate(
        [mixacc[:, LANES:], jnp.zeros((192, CF), F32)], axis=1
    )
    grads[HEAD_ROW : HEAD_ROW + COUT] = jnp.concatenate(
        [head_sum, jnp.zeros((COUT, CF), F32)], axis=1
    )
    grads[HEAD_ROW + COUT :] = jnp.zeros((GRAD_ROWS - HEAD_ROW - COUT, LANES), F32)

    half = GRAD_ROWS // 2
    piece = half // chips

    def rows(start, size):
        return pl.ds(pl.multiple_of(start, 8), size)

    def part(number, source, target, peer):
        return pltpu.make_async_remote_copy(
            src_ref=source, dst_ref=target,
            send_sem=sum_send.at[number], recv_sem=sum_recv.at[number],
            device_id=peer, device_id_type=MESH,
        )

    base = core * half
    own = rows(here_chip * piece, piece)
    own_final = final.at[rows(base + here_chip * piece, piece)]

    def spread_part(k):
        number, peer = chip_at(k)
        return part(k, total.at[rows(number * piece, piece)], parts.at[k - 1], peer)

    def share_part(k):
        return part(chips + k, own_final, own_final, chip_at(k)[1])

    first = part(0, grads.at[rows((1 - core) * half, half)], other, core_peer)
    first.start()
    sample_next()
    first.wait_recv()
    total[...] = grads[rows(base, half)] + other[...]

    pl.loop(1, chips)(lambda k: spread_part(k).start())
    sample_next()
    pl.loop(1, chips)(lambda k: spread_part(k).wait_recv())
    final[rows(base + here_chip * piece, piece)] = total[own] + jnp.sum(parts[...], axis=0)

    pl.loop(1, chips)(lambda k: share_part(k).start())
    sample_next()
    pl.loop(1, chips)(lambda k: share_part(k).wait_recv())
    half_final = final.at[rows(base, half)]
    last = part(chips, half_final, half_final, core_peer)
    last.start()
    last.wait_recv()

    up_ref[...] = final[:MIX_ROW]
    for col_tap in range(3):
        for row_tap in range(3):
            at = MIX_ROW + (col_tap // 2) * 192 + row_tap * CF
            lanes = (col_tap % 2) * CF
            to = (col_tap * 3 + row_tap) * CF
            mix_ref[to : to + CF] = final[at : at + CF, lanes : lanes + CF]
    headg_ref[...] = final[HEAD_ROW : HEAD_ROW + COUT, :CF]
    first.wait_send()
    last.wait_send()

    @pl.loop(1, chips)
    def _(k):
        spread_part(k).wait_send()
        share_part(k).wait_send()

    for copy in copies:
        copy.wait_send()


def move_kernel(*refs):
    count = len(refs) // 2
    for k in range(count):
        refs[count + k][...] = refs[k][...]


def vmem(count):
    return [pl.BlockSpec(memory_space=pltpu.VMEM)] * count


def per_device(nf, npat, coarse, w_up, w_mix, w_head, send_index, slot_ids, fractions, head_cot):
    points = slot_ids.shape[1]
    run = COLS * COUT
    chips, half = nf * npat // 2, GRAD_ROWS // 2
    scratch = [
        pltpu.VMEM((COLS + 3, CIN, LANES), BF16),
        pltpu.VMEM((COLS + 2, CIN, LANES), BF16),
        pltpu.VMEM((len(NEIGHBOURS) + 1, CIN, LANES), BF16),
        pltpu.VMEM((6 * CF, 2 * CIN), BF16),
        pltpu.VMEM((3 * CF, 3 * CF), BF16),
        pltpu.VMEM((3 * CF, 3 * CF), BF16),
        pltpu.VMEM((36, CF, 256), BF16),
        pltpu.VMEM((36, CF, 256), F32),
        pltpu.VMEM((32, CF, 256), F32),
        pltpu.VMEM((32, CF, 256), BF16),
        pltpu.VMEM((32, COUT, 256), F32),
        pltpu.VMEM((16, 16, 256), BF16),
        pltpu.VMEM((32, 16, 256), BF16),
        pltpu.VMEM((4 * run, 256), F32),
        pltpu.VMEM((3, run, 256), F32),
        pltpu.VMEM((48, COUT, 256), F32),
        pltpu.VMEM((34, CF, 256), BF16),
        pltpu.VMEM((CF, LANES), F32),
        pltpu.VMEM((len(ROW_NEIGHBOURS) + 1, CF, LANES), BF16),
        pltpu.VMEM((34, 3 * CF, 256), F32),
        pltpu.VMEM((3 * CF, 3 * CF), F32),
        pltpu.VMEM((3, 2 * CF, 2 * CIN), F32),
        pltpu.SMEM((4, LANES), jnp.int32),
        pltpu.SemaphoreType.DMA,
        pltpu.VMEM((GRAD_ROWS, LANES), F32),
        pltpu.VMEM((GRAD_ROWS, LANES), F32),
        pltpu.VMEM((half, LANES), F32),
        pltpu.VMEM((half, LANES), F32),
        pltpu.VMEM((chips - 1, half // chips, LANES), F32),
        pltpu.SemaphoreType.DMA((2 * chips,)),
        pltpu.SemaphoreType.DMA((2 * chips,)),
        pltpu.SemaphoreType.DMA((24,)),
        pltpu.SemaphoreType.DMA((24,)),
    ]
    head, up, mix, head_grad = pl.pallas_call(
        functools.partial(local_kernel, nf, npat),
        out_shape=(
            jax.ShapeDtypeStruct((COUT, points), F32),
            jax.ShapeDtypeStruct((9 * CF, CIN), F32),
            jax.ShapeDtypeStruct((9 * CF, CF), F32),
            jax.ShapeDtypeStruct((COUT, CF), F32),
        ),
        in_specs=[pl.BlockSpec(memory_space=pl.ANY)] + vmem(7),
        out_specs=tuple(vmem(4)),
        scratch_shapes=scratch,
        compiler_params=pltpu.CompilerParams(
            collective_id=0, has_side_effects=True, vmem_limit_bytes=56 * 2**20
        ),
        name="local",
    )(send_index, coarse, w_up, w_mix, w_head, slot_ids, fractions, head_cot)

    results = (head, up, mix, head_grad)
    head, up, mix, head_grad = pl.pallas_call(
        move_kernel,
        out_shape=tuple(jax.ShapeDtypeStruct(one.shape, one.dtype) for one in results),
        in_specs=vmem(4),
        out_specs=tuple(vmem(4)),
        compiler_params=pltpu.CompilerParams(vmem_limit_bytes=56 * 2**20),
        name="move",
    )(*results)
    return head, up.reshape(3, 3, CF, CIN), mix.reshape(3, 3, CF, CF), head_grad


def solution(mesh):
    placed = (
        P(None, "patch", "face"),
        P(),
        P(),
        P(),
        P("face", "patch", None),
        P(None, ("face", "patch")),
        P(None, ("face", "patch")),
        P(None, ("face", "patch")),
    )
    return jax.shard_map(
        functools.partial(per_device, mesh.shape["face"], mesh.shape["patch"]),
        mesh=mesh,
        in_specs=placed,
        out_specs=(P(None, ("face", "patch")), P(), P(), P()),
        check_vma=False,
    )
```

```python
import functools

import jax
import jax.numpy as jnp
from jax import lax
from jax.experimental import pallas as pl
from jax.experimental.pallas import tpu as pltpu
from jax.sharding import PartitionSpec as P

MESH = pl.DeviceIdType.MESH
F32 = jnp.float32
BF16 = jnp.bfloat16

LANES = 128
CIN = 128
CF = 64
COUT = 8
COLS = 16
POINT_TILE = 2048
EARLY = 2
SAMPLE_CUTS = (2, 3, 6)
GRAD_ROWS = 1024
MIX_ROW = 9 * CF
HEAD_ROW = MIX_ROW + 6 * CF
NEIGHBOURS = tuple((df, dp) for df in (-1, 0, 1) for dp in (-1, 0, 1) if (df, dp) != (0, 0))
ROW_NEIGHBOURS = tuple(pair for pair in NEIGHBOURS if pair[0] != 0)


def dot(left, right):
    return lax.dot_general(left, right, (((1,), (0,)), ((), ())), preferred_element_type=F32)


def dot_nt(left, right):
    return lax.dot_general(left, right, (((1,), (1,)), ((), ())), preferred_element_type=F32)


def turn(value, steps):
    if isinstance(steps, int):
        steps = steps % LANES
        if steps == 0:
            return value
    return pltpu.roll(value, steps, axis=1)


def sigmoid(value):
    return 0.5 * jnp.tanh(0.5 * value) + 0.5


def row_weights(slot, along):
    width = slot.shape[1]
    larger = jnp.maximum(along, 1.0 - along)
    upper, lower = along / larger, (1.0 - along) / larger
    place = lax.broadcasted_iota(jnp.int32, (256, width), 0)
    natural = 2 * (place & 127) + (place >> 7)
    away = natural - (slot & 255)
    weight = jnp.where(away == 0, lower, jnp.where(away == 1, upper, 0.0))
    return weight.astype(BF16), larger


def local_kernel(
    nf, npat,
    send_ref, coarse_ref, wup_ref, wmix_ref, whead_ref,
    slot_ref, frac_ref, cot_ref,
    head_ref, up_ref, mix_ref, headg_ref,
    ext, exts, edges, upw, mixw, backw, hid, slope1, slope2, feat, gown, gsend, table,
    sacc, srecv, pad, sc, strip, strips, zbuf, mixacc, upacc, starts, start_sem,
    grads, final, total, other, parts, sum_send, sum_recv,
    send_sem, recv_sem,
):
    me_f, me_p = lax.axis_index("face"), lax.axis_index("patch")

    def device(df, dp):
        return (lax.rem(me_f + df + nf, nf), lax.rem(me_p + dp + npat, npat))

    start_copy = pltpu.make_async_copy(send_ref.at[0, :, pl.ds(0, LANES)], starts, start_sem)
    start_copy.start()
    barrier = pltpu.get_barrier_semaphore()
    partners = NEIGHBOURS + ((0, 2), (0, -2))
    chips = nf * npat // 2
    core = lax.rem(me_p, 2)
    here_chip = me_f * (npat // 2) + me_p // 2
    core_peer = (me_f, me_p + 1 - 2 * core)

    def chip_at(k):
        face = lax.rem(me_f + k // (npat // 2), nf)
        pair = lax.rem(me_p // 2 + k % (npat // 2), npat // 2)
        return face * (npat // 2) + pair, (face, 2 * pair + core)

    for df, dp in partners:
        pl.semaphore_signal(barrier, inc=1, device_id=device(df, dp), device_id_type=MESH)
    pl.semaphore_signal(barrier, inc=1, device_id=core_peer, device_id_type=MESH)

    @pl.loop(1, chips)
    def _(k):
        pl.semaphore_signal(barrier, inc=1, device_id=chip_at(k)[1], device_id_type=MESH)


    copies = []

    def send(source, target, offset):
        number = len(copies)
        copy = pltpu.make_async_remote_copy(
            src_ref=source, dst_ref=target,
            send_sem=send_sem.at[number], recv_sem=recv_sem.at[number],
            device_id=device(*offset), device_id_type=MESH,
        )
        copy.start()
        copies.append(copy)
        return copy

    lane = lax.broadcasted_iota(jnp.int32, (CIN, LANES), 1)
    lane64 = lane[:CF]
    ext[1 : COLS + 1] = jnp.swapaxes(coarse_ref[...], 0, 1)
    edge = jnp.zeros((CIN, LANES), F32)
    for j in range(COLS):
        column = ext[j + 1].astype(F32)
        edge = jnp.where(lane == j, turn(column, j), edge)
        edge = jnp.where(lane == COLS + j, turn(column, COLS + 1 + j), edge)
    edge_own = edges.at[len(NEIGHBOURS)]
    edge_own[...] = edge.astype(BF16)
    ext[COLS + 2] = jnp.zeros((CIN, LANES), BF16)
    for row_tap in range(3):
        low = slice(row_tap * CF, (row_tap + 1) * CF)
        high = slice((3 + row_tap) * CF, (4 + row_tap) * CF)
        upw[low, :CIN] = wup_ref[1, row_tap]
        upw[low, CIN:] = jnp.zeros((CF, CIN), BF16)
        upw[high, :CIN] = wup_ref[2, row_tap]
        upw[high, CIN:] = wup_ref[0, row_tap]
    mix_rows = [
        jnp.concatenate([wmix_ref[col_tap, row_tap].astype(F32) for col_tap in range(3)], axis=1)
        for row_tap in range(3)
    ]
    mixing = jnp.concatenate(mix_rows, axis=0)
    mixw[...] = mixing.astype(BF16)
    backw[...] = mixing.T.astype(BF16)

    sacc[...] = jnp.zeros_like(sacc)

    def scatter(step):
        here = pl.ds(pl.multiple_of(step * POINT_TILE, POINT_TILE), POINT_TILE)
        slot = slot_ref[0:1, here]
        along, across = frac_ref[0:1, here], frac_ref[1:2, here]
        rows, larger = row_weights(slot, along)
        cot = cot_ref[:, here] * larger
        near, far = cot * (1.0 - across), cot * across
        column = jnp.broadcast_to(slot >> 8, near.shape)[None]
        number = lax.broadcasted_iota(jnp.int32, (64,) + near.shape, 0)
        away = number - column
        terms = jnp.where(away == 0, near[None], jnp.where(away == 1, far[None], 0.0))
        sacc[...] += dot_nt(terms.reshape(64 * COUT, POINT_TILE).astype(BF16), rows)

    tiles = slot_ref.shape[1] // POINT_TILE
    early = tiles * EARLY // 8
    pl.loop(0, early)(scatter)
    pl.semaphore_wait(barrier, len(partners) + chips)
    coarse_copies = [
        send(ext.at[1], ext.at[COLS + 1], (0, -1)),
        send(ext.at[COLS], ext.at[0], (0, 1)),
    ]
    for number, offset in enumerate(NEIGHBOURS):
        coarse_copies.append(send(edge_own, edges.at[number], offset))

    pl.loop(early, tiles)(scatter)

    run = COLS * COUT
    pad[0:16] = jnp.zeros((16, COUT, 256), F32)
    pad[16:32] = sacc[2 * run : 3 * run].reshape(16, COUT, 256)
    pad[32:48] = jnp.zeros((16, COUT, 256), F32)
    back_copies = [
        send(sacc.at[0:run], srecv.at[0], (0, 2)),
        send(sacc.at[run : 2 * run], srecv.at[1], (0, 1)),
        send(sacc.at[3 * run : 4 * run], srecv.at[2], (0, -1)),
    ]

    for copy in coarse_copies:
        copy.wait_recv()
    above = jnp.where(me_f > 0, 1.0, 0.0).astype(F32)
    below = jnp.where(me_f < nf - 1, 1.0, 0.0).astype(F32)

    def arrived(buffer, df, dp):
        pairs = NEIGHBOURS if buffer is edges else ROW_NEIGHBOURS
        return buffer[pairs.index((-df, -dp))].astype(F32)

    def between(low, high, index):
        return jnp.logical_and(index >= low, index < high)

    top = jnp.where(between(1, 17, lane), turn(arrived(edges, -1, 0), -15), 0.0)
    top = jnp.where(lane == 0, turn(arrived(edges, -1, -1), -31), top)
    top = jnp.where(lane == 17, turn(arrived(edges, -1, 1), 1), top) * above
    first_row = jnp.where(between(33, 49, lane), turn(edge, 33), 0.0)
    first_row = jnp.where(lane == 32, turn(arrived(edges, 0, -1), 17), first_row)
    first_row = jnp.where(lane == 49, turn(arrived(edges, 0, 1), 49), first_row)
    bottom = jnp.where(between(65, 81, lane), turn(arrived(edges, 1, 0), 65), 0.0)
    bottom = jnp.where(lane == 64, turn(arrived(edges, 1, -1), 49), bottom)
    bottom = jnp.where(lane == 81, turn(arrived(edges, 1, 1), 81), bottom) * below
    rim = top + first_row + bottom
    rim_pair = jnp.concatenate([rim, turn(rim, -1)], axis=0).astype(BF16)
    rim_out = dot(upw[...], rim_pair)
    rim_hidden = []
    for parity in range(2):
        part = rim_out[parity * 192 : (parity + 1) * 192]
        upper = part[128:192] + turn(part[0:64], -32)
        value = jnp.where(lane64 < 32, upper * above, jnp.where(between(64, 96, lane64), part[64:128], 0.0))
        rim_hidden.append(value * sigmoid(value))
    even_rim, odd_rim = rim_hidden
    mix_rim = [
        dot(mixw[...], jnp.concatenate([turn(odd_rim, 1), even_rim, odd_rim], axis=0).astype(BF16)),
        dot(mixw[...], jnp.concatenate([even_rim, odd_rim, turn(even_rim, -1)], axis=0).astype(BF16)),
    ]

    @pl.loop(0, 9, unroll=9)
    def _(step):
        t = 2 * step
        pair = [ext[pl.ds(t + k, 2)].reshape(2 * CIN, LANES) for k in range(2)]
        out = dot(upw[...], jnp.concatenate(pair, axis=1))
        for k in range(2):
            here = t + k
            for parity in range(2):
                part = out[parity * 192 : (parity + 1) * 192, k * LANES : (k + 1) * LANES]
                entering = turn(rim_out[parity * 192 : parity * 192 + 64], 63 - here)
                odd = part[128:192] + jnp.where(lane64 == 127, entering, turn(part[0:64], -1))
                value = jnp.concatenate([part[64:128], odd], axis=1)
                sigma = sigmoid(value)
                hid[2 * here + parity] = (value * sigma).astype(BF16)
                slope1[2 * here + parity] = sigma * (1.0 + value * (1.0 - sigma))
            shifted = turn(ext[here].astype(F32), -1)
            exts[here] = jnp.where(lane == 127, turn(rim, 63 - here), shifted).astype(BF16)

    weight = whead_ref[...]
    weight_high = weight.astype(BF16).astype(F32)
    head_pair = jnp.concatenate([weight_high, weight - weight_high], axis=0).astype(BF16)

    def mix_step(j):
        values = []
        for parity in range(2):
            q = 2 * j + parity
            out = dot(mixw[...], hid[pl.ds(q + 1, 3)].reshape(192, 256))
            low, mid, high = out[0:64], out[64:128], out[128:192]
            first = turn(mix_rim[parity][0:64], 127 - j)
            last = turn(mix_rim[parity][128:192], 62 - j)
            even = jnp.where(lane64 == 0, first, turn(low[:, LANES:], 1)) + mid[:, :LANES] + high[:, LANES:]
            odd = low[:, :LANES] + mid[:, LANES:] + jnp.where(lane64 == 127, last, turn(high[:, :LANES], -1))
            value = jnp.concatenate([even, odd], axis=1)
            sigma = sigmoid(value)
            feature = (value * sigma).astype(BF16)
            feat[q] = feature
            slope2[q] = sigma * (1.0 + value * (1.0 - sigma))
            both = dot(head_pair, feature)
            point_value = both[0:8] + both[8:16]
            gown[q] = point_value
            values.append(point_value)
        gsend[j] = jnp.concatenate(values, axis=0).astype(BF16)

    pl.loop(0, 8, unroll=8)(mix_step)
    value_copies = [
        send(gsend.at[0:8], table.at[0:8], (0, -2)),
        send(gsend.at[0:8], table.at[8:16], (0, -1)),
    ]
    pl.loop(8, 16, unroll=8)(mix_step)
    value_copies.append(send(gsend.at[8:16], table.at[24:32], (0, 1)))

    start_copy.wait()
    start = starts[2, 0] // 256
    for k in range(8):
        pair = [gown[start + 2 * k], gown[start + 2 * k + 1]]
        table[16 + k] = jnp.concatenate(pair, axis=0).astype(BF16)

    for copy in back_copies:
        copy.wait_recv()
    weight_t = whead_ref[...].T
    high_t = weight_t.astype(BF16).astype(F32)
    weight_three = jnp.concatenate([high_t, weight_t - high_t, high_t], axis=1).astype(BF16)
    strip[...] = jnp.zeros_like(strip)

    def cot_step(q, total, head_sum):
        high = total.astype(BF16).astype(F32)
        low = total - high
        fine = dot(weight_three, jnp.concatenate([high, high, low], axis=0).astype(BF16))
        value = fine * slope2[q]
        sc[q + 1] = value.astype(BF16)
        kept = jnp.where(lane64 == q, turn(value[:, :LANES], q), strip[...])
        strip[...] = jnp.where(lane64 == q + 32, turn(value[:, LANES:], q + 33), kept)
        both = dot_nt(jnp.concatenate([high, low], axis=0).astype(BF16), feat[q])
        return head_sum + both[0:8] + both[8:16]

    def row_of(number, q):
        return srecv[number, pl.ds(pl.multiple_of(q * COUT, COUT), COUT), :]

    def cot_low(q, head_sum):
        total = row_of(0, q) + row_of(1, q) + pad[16 + q - start]
        return cot_step(q, total, head_sum)

    def cot_high(q, head_sum):
        total = row_of(2, q - 16) + pad[16 + q - start]
        return cot_step(q, total, head_sum)

    head_sum = lax.fori_loop(0, 16, cot_low, jnp.zeros((COUT, CF), F32), unroll=8)
    head_sum = lax.fori_loop(16, 32, cot_high, head_sum, unroll=8)
    strips_own = strips.at[len(ROW_NEIGHBOURS)]
    strips_own[...] = strip[...].astype(BF16)
    cot_copies = [
        send(sc.at[1], sc.at[33], (0, -1)),
        send(sc.at[32], sc.at[0], (0, 1)),
    ]
    for number, offset in enumerate(ROW_NEIGHBOURS):
        cot_copies.append(send(strips_own, strips.at[number], offset))

    for copy in value_copies:
        copy.wait_recv()

    def sample(step):
        here = pl.ds(pl.multiple_of(step * POINT_TILE, POINT_TILE), POINT_TILE)
        slot = slot_ref[0:1, here]
        along, across = frac_ref[0:1, here], frac_ref[1:2, here]
        rows, larger = row_weights(slot, along)
        columns = dot(table[...].reshape(64 * COUT, 256), rows).reshape(64, COUT, POINT_TILE)
        column = jnp.broadcast_to(slot >> 8, (COUT, POINT_TILE))[None]
        number = lax.broadcasted_iota(jnp.int32, (64, COUT, POINT_TILE), 0)
        away = number - column
        near = jnp.broadcast_to((1.0 - across) * larger, (COUT, POINT_TILE))[None]
        far = jnp.broadcast_to(across * larger, (COUT, POINT_TILE))[None]
        weights = jnp.where(away == 0, near, jnp.where(away == 1, far, 0.0))
        head_ref[:, here] = jnp.sum(weights * columns, axis=0)

    tiles = slot_ref.shape[1] // POINT_TILE
    cuts = [0] + [tiles * part // 8 for part in SAMPLE_CUTS] + [tiles]
    segments = iter(zip(cuts[:-1], cuts[1:]))

    def sample_next():
        first, last = next(segments)
        pl.loop(first, last)(sample)

    sample_next()

    for copy in cot_copies:
        copy.wait_recv()
    upper = jnp.where(between(1, 33, lane64), turn(arrived(strips, -1, 0), -31), 0.0)
    upper = jnp.where(lane64 == 0, turn(arrived(strips, -1, -1), -63), upper)
    upper = jnp.where(lane64 == 33, turn(arrived(strips, -1, 1), 1), upper) * above
    lower = jnp.where(between(65, 97, lane64), turn(arrived(strips, 1, 0), 65), 0.0)
    lower = jnp.where(lane64 == 64, turn(arrived(strips, 1, -1), 33), lower)
    lower = jnp.where(lane64 == 97, turn(arrived(strips, 1, 1), 97), lower) * below
    cot_rim = upper + lower

    def back_step(w):
        value = sc[w].astype(F32)
        even, odd = value[:, :LANES], value[:, LANES:]
        last = jnp.where(lane64 == 127, turn(cot_rim, 63 - w), turn(even, -1))
        first = jnp.where(lane64 == 0, turn(cot_rim, LANES - w), turn(odd, 1))
        taps = jnp.concatenate(
            [jnp.concatenate([odd, last], axis=1), value, jnp.concatenate([first, even], axis=1)],
            axis=0,
        ).astype(BF16)
        zbuf[w] = dot(backw[...], taps)
        return taps

    mixacc[...] = jnp.zeros_like(mixacc)
    back_step(0)

    @pl.loop(1, 33, unroll=8)
    def _(w):
        taps = back_step(w)
        mixacc[...] += dot_nt(taps, hid[pl.ds(w, 3)].reshape(192, 256))

    back_step(33)

    upacc[...] = jnp.zeros_like(upacc)

    @pl.loop(0, 8, unroll=8)
    def _(step):
        evens, odds = [], []
        for k in range(2):
            even_parts, odd_parts = [], []
            for parity in range(2):
                q = 4 * step + 2 * k + parity
                total = zbuf[q + 2, 0:64] + zbuf[q + 1, 64:128] + zbuf[q, 128:192]
                value = (total * slope1[q + 2]).astype(BF16)
                even_parts.append(value[:, :LANES])
                odd_parts.append(value[:, LANES:])
            evens.append(jnp.concatenate(even_parts, axis=0))
            odds.append(jnp.concatenate(odd_parts, axis=0))
        even = jnp.concatenate(evens, axis=1)
        odd = jnp.concatenate(odds, axis=1)

        def window(buffer):
            pair = [buffer[pl.ds(2 * step + 1 + k, 2)].reshape(2 * CIN, LANES) for k in range(2)]
            return jnp.concatenate(pair, axis=1)

        plain, moved = window(ext), window(exts)
        upacc[0] += dot_nt(odd, moved)
        upacc[1] += dot_nt(even, plain)
        upacc[2] += dot_nt(odd, plain)

    for row_tap in range(3):
        for col_tap, rows, lanes in ((0, 64, 128), (1, 0, 0), (2, 64, 0)):
            at = (col_tap * 3 + row_tap) * CF
            grads[at : at + CF] = upacc[row_tap, rows : rows + CF, lanes : lanes + LANES]
    grads[MIX_ROW : MIX_ROW + 192] = mixacc[:, :LANES]
    grads[MIX_ROW + 192 : HEAD_ROW] = jnp.concatenate(
        [mixacc[:, LANES:], jnp.zeros((192, CF), F32)], axis=1
    )
    grads[HEAD_ROW : HEAD_ROW + COUT] = jnp.concatenate(
        [head_sum, jnp.zeros((COUT, CF), F32)], axis=1
    )
    grads[HEAD_ROW + COUT :] = jnp.zeros((GRAD_ROWS - HEAD_ROW - COUT, LANES), F32)

    half = GRAD_ROWS // 2
    piece = half // chips

    def rows(start, size):
        return pl.ds(pl.multiple_of(start, 8), size)

    def part(number, source, target, peer):
        return pltpu.make_async_remote_copy(
            src_ref=source, dst_ref=target,
            send_sem=sum_send.at[number], recv_sem=sum_recv.at[number],
            device_id=peer, device_id_type=MESH,
        )

    base = core * half
    own = rows(here_chip * piece, piece)
    own_final = final.at[rows(base + here_chip * piece, piece)]

    def spread_part(k):
        number, peer = chip_at(k)
        return part(k, total.at[rows(number * piece, piece)], parts.at[k - 1], peer)

    def share_part(k):
        return part(chips + k, own_final, own_final, chip_at(k)[1])

    first = part(0, grads.at[rows((1 - core) * half, half)], other, core_peer)
    first.start()
    sample_next()
    first.wait_recv()
    total[...] = grads[rows(base, half)] + other[...]

    pl.loop(1, chips)(lambda k: spread_part(k).start())
    sample_next()
    pl.loop(1, chips)(lambda k: spread_part(k).wait_recv())
    final[rows(base + here_chip * piece, piece)] = total[own] + jnp.sum(parts[...], axis=0)

    pl.loop(1, chips)(lambda k: share_part(k).start())
    sample_next()
    pl.loop(1, chips)(lambda k: share_part(k).wait_recv())
    half_final = final.at[rows(base, half)]
    last = part(chips, half_final, half_final, core_peer)
    last.start()
    last.wait_recv()

    up_ref[...] = final[:MIX_ROW]
    for col_tap in range(3):
        for row_tap in range(3):
            at = MIX_ROW + (col_tap // 2) * 192 + row_tap * CF
            lanes = (col_tap % 2) * CF
            to = (col_tap * 3 + row_tap) * CF
            mix_ref[to : to + CF] = final[at : at + CF, lanes : lanes + CF]
    headg_ref[...] = final[HEAD_ROW : HEAD_ROW + COUT, :CF]
    first.wait_send()
    last.wait_send()

    @pl.loop(1, chips)
    def _(k):
        spread_part(k).wait_send()
        share_part(k).wait_send()

    for copy in copies:
        copy.wait_send()


def move_kernel(*refs):
    count = len(refs) // 2
    for k in range(count):
        refs[count + k][...] = refs[k][...]


def vmem(count):
    return [pl.BlockSpec(memory_space=pltpu.VMEM)] * count


def per_device(nf, npat, coarse, w_up, w_mix, w_head, send_index, slot_ids, fractions, head_cot):
    points = slot_ids.shape[1]
    run = COLS * COUT
    chips, half = nf * npat // 2, GRAD_ROWS // 2
    scratch = [
        pltpu.VMEM((COLS + 3, CIN, LANES), BF16),
        pltpu.VMEM((COLS + 2, CIN, LANES), BF16),
        pltpu.VMEM((len(NEIGHBOURS) + 1, CIN, LANES), BF16),
        pltpu.VMEM((6 * CF, 2 * CIN), BF16),
        pltpu.VMEM((3 * CF, 3 * CF), BF16),
        pltpu.VMEM((3 * CF, 3 * CF), BF16),
        pltpu.VMEM((36, CF, 256), BF16),
        pltpu.VMEM((36, CF, 256), F32),
        pltpu.VMEM((32, CF, 256), F32),
        pltpu.VMEM((32, CF, 256), BF16),
        pltpu.VMEM((32, COUT, 256), F32),
        pltpu.VMEM((16, 16, 256), BF16),
        pltpu.VMEM((32, 16, 256), BF16),
        pltpu.VMEM((4 * run, 256), F32),
        pltpu.VMEM((3, run, 256), F32),
        pltpu.VMEM((48, COUT, 256), F32),
        pltpu.VMEM((34, CF, 256), BF16),
        pltpu.VMEM((CF, LANES), F32),
        pltpu.VMEM((len(ROW_NEIGHBOURS) + 1, CF, LANES), BF16),
        pltpu.VMEM((34, 3 * CF, 256), F32),
        pltpu.VMEM((3 * CF, 3 * CF), F32),
        pltpu.VMEM((3, 2 * CF, 2 * CIN), F32),
        pltpu.SMEM((4, LANES), jnp.int32),
        pltpu.SemaphoreType.DMA,
        pltpu.VMEM((GRAD_ROWS, LANES), F32),
        pltpu.VMEM((GRAD_ROWS, LANES), F32),
        pltpu.VMEM((half, LANES), F32),
        pltpu.VMEM((half, LANES), F32),
        pltpu.VMEM((chips - 1, half // chips, LANES), F32),
        pltpu.SemaphoreType.DMA((2 * chips,)),
        pltpu.SemaphoreType.DMA((2 * chips,)),
        pltpu.SemaphoreType.DMA((24,)),
        pltpu.SemaphoreType.DMA((24,)),
    ]
    head, up, mix, head_grad = pl.pallas_call(
        functools.partial(local_kernel, nf, npat),
        out_shape=(
            jax.ShapeDtypeStruct((COUT, points), F32),
            jax.ShapeDtypeStruct((9 * CF, CIN), F32),
            jax.ShapeDtypeStruct((9 * CF, CF), F32),
            jax.ShapeDtypeStruct((COUT, CF), F32),
        ),
        in_specs=[pl.BlockSpec(memory_space=pl.ANY)] + vmem(7),
        out_specs=tuple(vmem(4)),
        scratch_shapes=scratch,
        compiler_params=pltpu.CompilerParams(
            collective_id=0, has_side_effects=True, vmem_limit_bytes=56 * 2**20
        ),
        name="local",
    )(send_index, coarse, w_up, w_mix, w_head, slot_ids, fractions, head_cot)

    results = (head, up, mix, head_grad)
    head, up, mix, head_grad = pl.pallas_call(
        move_kernel,
        out_shape=tuple(jax.ShapeDtypeStruct(one.shape, one.dtype) for one in results),
        in_specs=vmem(4),
        out_specs=tuple(vmem(4)),
        compiler_params=pltpu.CompilerParams(vmem_limit_bytes=56 * 2**20),
        name="move",
    )(*results)
    return head, up.reshape(3, 3, CF, CIN), mix.reshape(3, 3, CF, CF), head_grad


def solution(mesh):
    placed = (
        P(None, "patch", "face"),
        P(),
        P(),
        P(),
        P("face", "patch", None),
        P(None, ("face", "patch")),
        P(None, ("face", "patch")),
        P(None, ("face", "patch")),
    )
    return jax.shard_map(
        functools.partial(per_device, mesh.shape["face"], mesh.shape["patch"]),
        mesh=mesh,
        in_specs=placed,
        out_specs=(P(None, ("face", "patch")), P(), P(), P()),
        check_vma=False,
    )
```

```python
import functools

import jax
import jax.numpy as jnp
from jax import lax
from jax.experimental import pallas as pl
from jax.experimental.pallas import tpu as pltpu
from jax.sharding import PartitionSpec as P

MESH = pl.DeviceIdType.MESH
F32 = jnp.float32
BF16 = jnp.bfloat16

LANES = 128
CIN = 128
CF = 64
COUT = 8
COLS = 16
POINT_TILE = 2048
EARLY = 2
SAMPLE_CUTS = (2, 3, 6)
GRAD_ROWS = 1024
MIX_ROW = 9 * CF
HEAD_ROW = MIX_ROW + 6 * CF
UP_HALF = MIX_ROW // 2
NEIGHBOURS = tuple((df, dp) for df in (-1, 0, 1) for dp in (-1, 0, 1) if (df, dp) != (0, 0))
ROW_NEIGHBOURS = tuple(pair for pair in NEIGHBOURS if pair[0] != 0)


def placed_rows(start, size):
    half = GRAD_ROWS // 2
    middle = MIX_ROW + half - UP_HALF
    runs = ((0, UP_HALF, 0), (UP_HALF, MIX_ROW, half), (MIX_ROW, middle, UP_HALF), (middle, GRAD_ROWS, half + UP_HALF))
    found = []
    for low, high, place in runs:
        first, last = max(low, start), min(high, start + size)
        if first < last:
            found.append((first, last - first, place + first - low))
    return found


def dot(left, right):
    return lax.dot_general(left, right, (((1,), (0,)), ((), ())), preferred_element_type=F32)


def dot_nt(left, right):
    return lax.dot_general(left, right, (((1,), (1,)), ((), ())), preferred_element_type=F32)


def turn(value, steps):
    if isinstance(steps, int):
        steps = steps % LANES
        if steps == 0:
            return value
    return pltpu.roll(value, steps, axis=1)


def sigmoid(value):
    return 0.5 * jnp.tanh(0.5 * value) + 0.5


def row_weights(slot, along):
    width = slot.shape[1]
    larger = jnp.maximum(along, 1.0 - along)
    upper, lower = along / larger, (1.0 - along) / larger
    place = lax.broadcasted_iota(jnp.int32, (256, width), 0)
    natural = 2 * (place & 127) + (place >> 7)
    away = natural - (slot & 255)
    weight = jnp.where(away == 0, lower, jnp.where(away == 1, upper, 0.0))
    return weight.astype(BF16), larger


def local_kernel(
    nf, npat,
    send_ref, coarse_ref, wup_ref, wmix_ref, whead_ref,
    slot_ref, frac_ref, cot_ref,
    head_ref, up_ref, mix_ref, headg_ref,
    ext, exts, edges, upw, mixw, backw, hid, slope1, slope2, feat, gown, gsend, table,
    sacc, srecv, pad, sc, strip, strips, zbuf, mixacc, upacc, starts, start_sem,
    grads, final, total, other, parts, sum_send, sum_recv,
    send_sem, recv_sem,
):
    me_f, me_p = lax.axis_index("face"), lax.axis_index("patch")

    def device(df, dp):
        return (lax.rem(me_f + df + nf, nf), lax.rem(me_p + dp + npat, npat))

    start_copy = pltpu.make_async_copy(send_ref.at[0, :, pl.ds(0, LANES)], starts, start_sem)
    start_copy.start()
    barrier = pltpu.get_barrier_semaphore()
    partners = NEIGHBOURS + ((0, 2), (0, -2))
    chips = nf * npat // 2
    core = lax.rem(me_p, 2)
    here_chip = me_f * (npat // 2) + me_p // 2
    core_peer = (me_f, me_p + 1 - 2 * core)

    def chip_at(k):
        face = lax.rem(me_f + k // (npat // 2), nf)
        pair = lax.rem(me_p // 2 + k % (npat // 2), npat // 2)
        return face * (npat // 2) + pair, (face, 2 * pair + core)

    for df, dp in partners:
        pl.semaphore_signal(barrier, inc=1, device_id=device(df, dp), device_id_type=MESH)
    pl.semaphore_signal(barrier, inc=1, device_id=core_peer, device_id_type=MESH)

    @pl.loop(1, chips)
    def _(k):
        pl.semaphore_signal(barrier, inc=1, device_id=chip_at(k)[1], device_id_type=MESH)


    copies = []

    def send(source, target, offset):
        number = len(copies)
        copy = pltpu.make_async_remote_copy(
            src_ref=source, dst_ref=target,
            send_sem=send_sem.at[number], recv_sem=recv_sem.at[number],
            device_id=device(*offset), device_id_type=MESH,
        )
        copy.start()
        copies.append(copy)
        return copy

    lane = lax.broadcasted_iota(jnp.int32, (CIN, LANES), 1)
    lane64 = lane[:CF]
    ext[1 : COLS + 1] = jnp.swapaxes(coarse_ref[...], 0, 1)
    edge = jnp.zeros((CIN, LANES), F32)
    for j in range(COLS):
        column = ext[j + 1].astype(F32)
        edge = jnp.where(lane == j, turn(column, j), edge)
        edge = jnp.where(lane == COLS + j, turn(column, COLS + 1 + j), edge)
    edge_own = edges.at[len(NEIGHBOURS)]
    edge_own[...] = edge.astype(BF16)
    ext[COLS + 2] = jnp.zeros((CIN, LANES), BF16)
    for row_tap in range(3):
        low = slice(row_tap * CF, (row_tap + 1) * CF)
        high = slice((3 + row_tap) * CF, (4 + row_tap) * CF)
        upw[low, :CIN] = wup_ref[1, row_tap]
        upw[low, CIN:] = jnp.zeros((CF, CIN), BF16)
        upw[high, :CIN] = wup_ref[2, row_tap]
        upw[high, CIN:] = wup_ref[0, row_tap]
    mix_rows = [
        jnp.concatenate([wmix_ref[col_tap, row_tap].astype(F32) for col_tap in range(3)], axis=1)
        for row_tap in range(3)
    ]
    mixing = jnp.concatenate(mix_rows, axis=0)
    mixw[...] = mixing.astype(BF16)
    backw[...] = mixing.T.astype(BF16)

    sacc[...] = jnp.zeros_like(sacc)

    def scatter(step):
        here = pl.ds(pl.multiple_of(step * POINT_TILE, POINT_TILE), POINT_TILE)
        slot = slot_ref[0:1, here]
        along, across = frac_ref[0:1, here], frac_ref[1:2, here]
        rows, larger = row_weights(slot, along)
        cot = cot_ref[:, here] * larger
        near, far = cot * (1.0 - across), cot * across
        column = jnp.broadcast_to(slot >> 8, near.shape)[None]
        number = lax.broadcasted_iota(jnp.int32, (64,) + near.shape, 0)
        away = number - column
        terms = jnp.where(away == 0, near[None], jnp.where(away == 1, far[None], 0.0))
        sacc[...] += dot_nt(terms.reshape(64 * COUT, POINT_TILE).astype(BF16), rows)

    tiles = slot_ref.shape[1] // POINT_TILE
    early = tiles * EARLY // 8
    pl.loop(0, early)(scatter)
    pl.semaphore_wait(barrier, len(partners) + chips)
    coarse_copies = [
        send(ext.at[1], ext.at[COLS + 1], (0, -1)),
        send(ext.at[COLS], ext.at[0], (0, 1)),
    ]
    for number, offset in enumerate(NEIGHBOURS):
        coarse_copies.append(send(edge_own, edges.at[number], offset))

    pl.loop(early, tiles)(scatter)

    run = COLS * COUT
    pad[0:16] = jnp.zeros((16, COUT, 256), F32)
    pad[16:32] = sacc[2 * run : 3 * run].reshape(16, COUT, 256)
    pad[32:48] = jnp.zeros((16, COUT, 256), F32)
    back_copies = [
        send(sacc.at[0:run], srecv.at[0], (0, 2)),
        send(sacc.at[run : 2 * run], srecv.at[1], (0, 1)),
        send(sacc.at[3 * run : 4 * run], srecv.at[2], (0, -1)),
    ]

    for copy in coarse_copies:
        copy.wait_recv()
    above = jnp.where(me_f > 0, 1.0, 0.0).astype(F32)
    below = jnp.where(me_f < nf - 1, 1.0, 0.0).astype(F32)

    def arrived(buffer, df, dp):
        pairs = NEIGHBOURS if buffer is edges else ROW_NEIGHBOURS
        return buffer[pairs.index((-df, -dp))].astype(F32)

    def between(low, high, index):
        return jnp.logical_and(index >= low, index < high)

    top = jnp.where(between(1, 17, lane), turn(arrived(edges, -1, 0), -15), 0.0)
    top = jnp.where(lane == 0, turn(arrived(edges, -1, -1), -31), top)
    top = jnp.where(lane == 17, turn(arrived(edges, -1, 1), 1), top) * above
    first_row = jnp.where(between(33, 49, lane), turn(edge, 33), 0.0)
    first_row = jnp.where(lane == 32, turn(arrived(edges, 0, -1), 17), first_row)
    first_row = jnp.where(lane == 49, turn(arrived(edges, 0, 1), 49), first_row)
    bottom = jnp.where(between(65, 81, lane), turn(arrived(edges, 1, 0), 65), 0.0)
    bottom = jnp.where(lane == 64, turn(arrived(edges, 1, -1), 49), bottom)
    bottom = jnp.where(lane == 81, turn(arrived(edges, 1, 1), 81), bottom) * below
    rim = top + first_row + bottom
    rim_pair = jnp.concatenate([rim, turn(rim, -1)], axis=0).astype(BF16)
    rim_out = dot(upw[...], rim_pair)
    rim_hidden = []
    for parity in range(2):
        part = rim_out[parity * 192 : (parity + 1) * 192]
        upper = part[128:192] + turn(part[0:64], -32)
        value = jnp.where(lane64 < 32, upper * above, jnp.where(between(64, 96, lane64), part[64:128], 0.0))
        rim_hidden.append(value * sigmoid(value))
    even_rim, odd_rim = rim_hidden
    mix_rim = [
        dot(mixw[...], jnp.concatenate([turn(odd_rim, 1), even_rim, odd_rim], axis=0).astype(BF16)),
        dot(mixw[...], jnp.concatenate([even_rim, odd_rim, turn(even_rim, -1)], axis=0).astype(BF16)),
    ]

    @pl.loop(0, 9, unroll=9)
    def _(step):
        t = 2 * step
        pair = [ext[pl.ds(t + k, 2)].reshape(2 * CIN, LANES) for k in range(2)]
        out = dot(upw[...], jnp.concatenate(pair, axis=1))
        for k in range(2):
            here = t + k
            for parity in range(2):
                part = out[parity * 192 : (parity + 1) * 192, k * LANES : (k + 1) * LANES]
                entering = turn(rim_out[parity * 192 : parity * 192 + 64], 63 - here)
                odd = part[128:192] + jnp.where(lane64 == 127, entering, turn(part[0:64], -1))
                value = jnp.concatenate([part[64:128], odd], axis=1)
                sigma = sigmoid(value)
                hid[2 * here + parity] = (value * sigma).astype(BF16)
                slope1[2 * here + parity] = sigma * (1.0 + value * (1.0 - sigma))
            shifted = turn(ext[here].astype(F32), -1)
            exts[here] = jnp.where(lane == 127, turn(rim, 63 - here), shifted).astype(BF16)

    weight = whead_ref[...]
    weight_high = weight.astype(BF16).astype(F32)
    head_pair = jnp.concatenate([weight_high, weight - weight_high], axis=0).astype(BF16)

    def mix_step(j):
        values = []
        for parity in range(2):
            q = 2 * j + parity
            out = dot(mixw[...], hid[pl.ds(q + 1, 3)].reshape(192, 256))
            low, mid, high = out[0:64], out[64:128], out[128:192]
            first = turn(mix_rim[parity][0:64], 127 - j)
            last = turn(mix_rim[parity][128:192], 62 - j)
            even = jnp.where(lane64 == 0, first, turn(low[:, LANES:], 1)) + mid[:, :LANES] + high[:, LANES:]
            odd = low[:, :LANES] + mid[:, LANES:] + jnp.where(lane64 == 127, last, turn(high[:, :LANES], -1))
            value = jnp.concatenate([even, odd], axis=1)
            sigma = sigmoid(value)
            feature = (value * sigma).astype(BF16)
            feat[q] = feature
            slope2[q] = sigma * (1.0 + value * (1.0 - sigma))
            both = dot(head_pair, feature)
            point_value = both[0:8] + both[8:16]
            gown[q] = point_value
            values.append(point_value)
        gsend[j] = jnp.concatenate(values, axis=0).astype(BF16)

    pl.loop(0, 8, unroll=8)(mix_step)
    value_copies = [
        send(gsend.at[0:8], table.at[0:8], (0, -2)),
        send(gsend.at[0:8], table.at[8:16], (0, -1)),
    ]
    pl.loop(8, 16, unroll=8)(mix_step)
    value_copies.append(send(gsend.at[8:16], table.at[24:32], (0, 1)))

    start_copy.wait()
    start = starts[2, 0] // 256
    for k in range(8):
        pair = [gown[start + 2 * k], gown[start + 2 * k + 1]]
        table[16 + k] = jnp.concatenate(pair, axis=0).astype(BF16)

    for copy in back_copies:
        copy.wait_recv()
    weight_t = whead_ref[...].T
    high_t = weight_t.astype(BF16).astype(F32)
    weight_three = jnp.concatenate([high_t, weight_t - high_t, high_t], axis=1).astype(BF16)
    strip[...] = jnp.zeros_like(strip)

    def cot_step(q, total, head_sum):
        high = total.astype(BF16).astype(F32)
        low = total - high
        fine = dot(weight_three, jnp.concatenate([high, high, low], axis=0).astype(BF16))
        value = fine * slope2[q]
        sc[q + 1] = value.astype(BF16)
        kept = jnp.where(lane64 == q, turn(value[:, :LANES], q), strip[...])
        strip[...] = jnp.where(lane64 == q + 32, turn(value[:, LANES:], q + 33), kept)
        both = dot_nt(jnp.concatenate([high, low], axis=0).astype(BF16), feat[q])
        return head_sum + both[0:8] + both[8:16]

    def row_of(number, q):
        return srecv[number, pl.ds(pl.multiple_of(q * COUT, COUT), COUT), :]

    def cot_low(q, head_sum):
        total = row_of(0, q) + row_of(1, q) + pad[16 + q - start]
        return cot_step(q, total, head_sum)

    def cot_high(q, head_sum):
        total = row_of(2, q - 16) + pad[16 + q - start]
        return cot_step(q, total, head_sum)

    head_sum = lax.fori_loop(0, 16, cot_low, jnp.zeros((COUT, CF), F32), unroll=8)
    head_sum = lax.fori_loop(16, 32, cot_high, head_sum, unroll=8)
    strips_own = strips.at[len(ROW_NEIGHBOURS)]
    strips_own[...] = strip[...].astype(BF16)
    cot_copies = [
        send(sc.at[1], sc.at[33], (0, -1)),
        send(sc.at[32], sc.at[0], (0, 1)),
    ]
    for number, offset in enumerate(ROW_NEIGHBOURS):
        cot_copies.append(send(strips_own, strips.at[number], offset))

    for copy in value_copies:
        copy.wait_recv()

    def sample(step):
        here = pl.ds(pl.multiple_of(step * POINT_TILE, POINT_TILE), POINT_TILE)
        slot = slot_ref[0:1, here]
        along, across = frac_ref[0:1, here], frac_ref[1:2, here]
        rows, larger = row_weights(slot, along)
        columns = dot(table[...].reshape(64 * COUT, 256), rows).reshape(64, COUT, POINT_TILE)
        column = jnp.broadcast_to(slot >> 8, (COUT, POINT_TILE))[None]
        number = lax.broadcasted_iota(jnp.int32, (64, COUT, POINT_TILE), 0)
        away = number - column
        near = jnp.broadcast_to((1.0 - across) * larger, (COUT, POINT_TILE))[None]
        far = jnp.broadcast_to(across * larger, (COUT, POINT_TILE))[None]
        weights = jnp.where(away == 0, near, jnp.where(away == 1, far, 0.0))
        head_ref[:, here] = jnp.sum(weights * columns, axis=0)

    tiles = slot_ref.shape[1] // POINT_TILE
    cuts = [0] + [tiles * part // 8 for part in SAMPLE_CUTS] + [tiles]
    segments = iter(zip(cuts[:-1], cuts[1:]))

    def sample_next():
        first, last = next(segments)
        pl.loop(first, last)(sample)

    sample_next()

    for copy in cot_copies:
        copy.wait_recv()
    upper = jnp.where(between(1, 33, lane64), turn(arrived(strips, -1, 0), -31), 0.0)
    upper = jnp.where(lane64 == 0, turn(arrived(strips, -1, -1), -63), upper)
    upper = jnp.where(lane64 == 33, turn(arrived(strips, -1, 1), 1), upper) * above
    lower = jnp.where(between(65, 97, lane64), turn(arrived(strips, 1, 0), 65), 0.0)
    lower = jnp.where(lane64 == 64, turn(arrived(strips, 1, -1), 33), lower)
    lower = jnp.where(lane64 == 97, turn(arrived(strips, 1, 1), 97), lower) * below
    cot_rim = upper + lower

    def back_step(w):
        value = sc[w].astype(F32)
        even, odd = value[:, :LANES], value[:, LANES:]
        last = jnp.where(lane64 == 127, turn(cot_rim, 63 - w), turn(even, -1))
        first = jnp.where(lane64 == 0, turn(cot_rim, LANES - w), turn(odd, 1))
        taps = jnp.concatenate(
            [jnp.concatenate([odd, last], axis=1), value, jnp.concatenate([first, even], axis=1)],
            axis=0,
        ).astype(BF16)
        zbuf[w] = dot(backw[...], taps)
        return taps

    mixacc[...] = jnp.zeros_like(mixacc)
    back_step(0)

    @pl.loop(1, 33, unroll=8)
    def _(w):
        taps = back_step(w)
        mixacc[...] += dot_nt(taps, hid[pl.ds(w, 3)].reshape(192, 256))

    back_step(33)

    half = GRAD_ROWS // 2
    piece = half // chips

    def rows(start, size):
        return pl.ds(pl.multiple_of(start, 8), size)

    def part(number, source, target, peer):
        return pltpu.make_async_remote_copy(
            src_ref=source, dst_ref=target,
            send_sem=sum_send.at[number], recv_sem=sum_recv.at[number],
            device_id=peer, device_id_type=MESH,
        )

    def half_part(number, start, size):
        source = grads.at[rows((1 - core) * half + start, size)]
        return part(number, source, other.at[start : start + size], core_peer)

    def put(at, value):
        for start, size, place in placed_rows(at, value.shape[0]):
            grads[place : place + size] = value[start - at : start - at + size]

    put(MIX_ROW, mixacc[:, :LANES])
    put(MIX_ROW + 192, jnp.concatenate([mixacc[:, LANES:], jnp.zeros((192, CF), F32)], axis=1))
    put(HEAD_ROW, jnp.concatenate([head_sum, jnp.zeros((COUT, CF), F32)], axis=1))
    put(HEAD_ROW + COUT, jnp.zeros((GRAD_ROWS - HEAD_ROW - COUT, LANES), F32))
    early_sum = half_part(0, UP_HALF, half - UP_HALF)
    early_sum.start()

    upacc[...] = jnp.zeros_like(upacc)

    @pl.loop(0, 8, unroll=8)
    def _(step):
        evens, odds = [], []
        for k in range(2):
            even_parts, odd_parts = [], []
            for parity in range(2):
                q = 4 * step + 2 * k + parity
                total = zbuf[q + 2, 0:64] + zbuf[q + 1, 64:128] + zbuf[q, 128:192]
                value = (total * slope1[q + 2]).astype(BF16)
                even_parts.append(value[:, :LANES])
                odd_parts.append(value[:, LANES:])
            evens.append(jnp.concatenate(even_parts, axis=0))
            odds.append(jnp.concatenate(odd_parts, axis=0))
        even = jnp.concatenate(evens, axis=1)
        odd = jnp.concatenate(odds, axis=1)

        def window(buffer):
            pair = [buffer[pl.ds(2 * step + 1 + k, 2)].reshape(2 * CIN, LANES) for k in range(2)]
            return jnp.concatenate(pair, axis=1)

        plain, moved = window(ext), window(exts)
        upacc[0] += dot_nt(odd, moved)
        upacc[1] += dot_nt(even, plain)
        upacc[2] += dot_nt(odd, plain)

    for row_tap in range(3):
        for col_tap, low, lanes in ((0, 64, 128), (1, 0, 0), (2, 64, 0)):
            put((col_tap * 3 + row_tap) * CF, upacc[row_tap, low : low + CF, lanes : lanes + LANES])

    base = core * half
    own = rows(here_chip * piece, piece)
    own_final = final.at[rows(base + here_chip * piece, piece)]

    def spread_part(k):
        number, peer = chip_at(k)
        return part(k, total.at[rows(number * piece, piece)], parts.at[k - 1], peer)

    def share_part(k):
        return part(chips + k, own_final, own_final, chip_at(k)[1])

    first = half_part(2 * chips, 0, UP_HALF)
    first.start()
    sample_next()
    first.wait_recv()
    early_sum.wait_recv()
    total[...] = grads[rows(base, half)] + other[...]

    pl.loop(1, chips)(lambda k: spread_part(k).start())
    sample_next()
    pl.loop(1, chips)(lambda k: spread_part(k).wait_recv())
    final[rows(base + here_chip * piece, piece)] = total[own] + jnp.sum(parts[...], axis=0)

    pl.loop(1, chips)(lambda k: share_part(k).start())
    sample_next()
    pl.loop(1, chips)(lambda k: share_part(k).wait_recv())
    half_final = final.at[rows(base, half)]
    last = part(chips, half_final, half_final, core_peer)
    last.start()
    last.wait_recv()

    for start, size, place in placed_rows(0, MIX_ROW):
        up_ref[start : start + size] = final[place : place + size]
    for col_tap in range(3):
        for row_tap in range(3):
            at = MIX_ROW + (col_tap // 2) * 192 + row_tap * CF
            lanes = (col_tap % 2) * CF
            to = (col_tap * 3 + row_tap) * CF
            for start, size, place in placed_rows(at, CF):
                here = to + start - at
                mix_ref[here : here + size] = final[place : place + size, lanes : lanes + CF]
    for start, size, place in placed_rows(HEAD_ROW, COUT):
        headg_ref[start - HEAD_ROW : start - HEAD_ROW + size] = final[place : place + size, :CF]
    first.wait_send()
    early_sum.wait_send()
    last.wait_send()

    @pl.loop(1, chips)
    def _(k):
        spread_part(k).wait_send()
        share_part(k).wait_send()

    for copy in copies:
        copy.wait_send()


def move_kernel(*refs):
    count = len(refs) // 2
    for k in range(count):
        refs[count + k][...] = refs[k][...]


def vmem(count):
    return [pl.BlockSpec(memory_space=pltpu.VMEM)] * count


def per_device(nf, npat, coarse, w_up, w_mix, w_head, send_index, slot_ids, fractions, head_cot):
    points = slot_ids.shape[1]
    run = COLS * COUT
    chips, half = nf * npat // 2, GRAD_ROWS // 2
    scratch = [
        pltpu.VMEM((COLS + 3, CIN, LANES), BF16),
        pltpu.VMEM((COLS + 2, CIN, LANES), BF16),
        pltpu.VMEM((len(NEIGHBOURS) + 1, CIN, LANES), BF16),
        pltpu.VMEM((6 * CF, 2 * CIN), BF16),
        pltpu.VMEM((3 * CF, 3 * CF), BF16),
        pltpu.VMEM((3 * CF, 3 * CF), BF16),
        pltpu.VMEM((36, CF, 256), BF16),
        pltpu.VMEM((36, CF, 256), F32),
        pltpu.VMEM((32, CF, 256), F32),
        pltpu.VMEM((32, CF, 256), BF16),
        pltpu.VMEM((32, COUT, 256), F32),
        pltpu.VMEM((16, 16, 256), BF16),
        pltpu.VMEM((32, 16, 256), BF16),
        pltpu.VMEM((4 * run, 256), F32),
        pltpu.VMEM((3, run, 256), F32),
        pltpu.VMEM((48, COUT, 256), F32),
        pltpu.VMEM((34, CF, 256), BF16),
        pltpu.VMEM((CF, LANES), F32),
        pltpu.VMEM((len(ROW_NEIGHBOURS) + 1, CF, LANES), BF16),
        pltpu.VMEM((34, 3 * CF, 256), F32),
        pltpu.VMEM((3 * CF, 3 * CF), F32),
        pltpu.VMEM((3, 2 * CF, 2 * CIN), F32),
        pltpu.SMEM((4, LANES), jnp.int32),
        pltpu.SemaphoreType.DMA,
        pltpu.VMEM((GRAD_ROWS, LANES), F32),
        pltpu.VMEM((GRAD_ROWS, LANES), F32),
        pltpu.VMEM((half, LANES), F32),
        pltpu.VMEM((half, LANES), F32),
        pltpu.VMEM((chips - 1, half // chips, LANES), F32),
        pltpu.SemaphoreType.DMA((2 * chips + 1,)),
        pltpu.SemaphoreType.DMA((2 * chips + 1,)),
        pltpu.SemaphoreType.DMA((24,)),
        pltpu.SemaphoreType.DMA((24,)),
    ]
    head, up, mix, head_grad = pl.pallas_call(
        functools.partial(local_kernel, nf, npat),
        out_shape=(
            jax.ShapeDtypeStruct((COUT, points), F32),
            jax.ShapeDtypeStruct((9 * CF, CIN), F32),
            jax.ShapeDtypeStruct((9 * CF, CF), F32),
            jax.ShapeDtypeStruct((COUT, CF), F32),
        ),
        in_specs=[pl.BlockSpec(memory_space=pl.ANY)] + vmem(7),
        out_specs=tuple(vmem(4)),
        scratch_shapes=scratch,
        compiler_params=pltpu.CompilerParams(
            collective_id=0, has_side_effects=True, vmem_limit_bytes=56 * 2**20
        ),
        name="local",
    )(send_index, coarse, w_up, w_mix, w_head, slot_ids, fractions, head_cot)

    results = (head, up, mix, head_grad)
    head, up, mix, head_grad = pl.pallas_call(
        move_kernel,
        out_shape=tuple(jax.ShapeDtypeStruct(one.shape, one.dtype) for one in results),
        in_specs=vmem(4),
        out_specs=tuple(vmem(4)),
        compiler_params=pltpu.CompilerParams(vmem_limit_bytes=56 * 2**20),
        name="move",
    )(*results)
    return head, up.reshape(3, 3, CF, CIN), mix.reshape(3, 3, CF, CF), head_grad


def solution(mesh):
    placed = (
        P(None, "patch", "face"),
        P(),
        P(),
        P(),
        P("face", "patch", None),
        P(None, ("face", "patch")),
        P(None, ("face", "patch")),
        P(None, ("face", "patch")),
    )
    return jax.shard_map(
        functools.partial(per_device, mesh.shape["face"], mesh.shape["patch"]),
        mesh=mesh,
        in_specs=placed,
        out_specs=(P(None, ("face", "patch")), P(), P(), P()),
        check_vma=False,
    )
```
